256 devices in a mesh: noise: 16 (over z_lo, x), qi: 2 (over core), kj: 8 (over z_hi, y).
Axes of the slice: x: 4, y: 4, z: 8 (z_hi: 2, z_lo: 4; z = z_hi * 4 + z_lo), core: 2. Of those that a mesh axis runs over, the one named last changes fastest.
Arguments:
- pair_rep: bfloat16 [512, 2, 256, 128], P('qi', None, 'kj'), may hold values from -6 to 6
- query_rows: bfloat16 [16, 512, 768], P('noise', 'qi'), may hold values from -10 to 10
- key_rows: bfloat16 [16, 2, 256, 768], P('noise', None, 'kj'), may hold values from -10 to 10
- value_rows: bfloat16 [16, 2, 256, 768], P('noise', None, 'kj'), may hold values from -6 to 6
- output_grad: bfloat16 [16, 512, 768], P('noise', 'qi'), may hold values from -96 to 96
- gain_first: float32 [128], replicated, may hold values from 0.5 to 1.5
- gate_weight: bfloat16 [128, 512], replicated, may hold values from -0.5 to 0.5
- up_weight: bfloat16 [128, 512], replicated, may hold values from -0.5 to 0.5
- down_weight: bfloat16 [512, 128], replicated, may hold values from -0.25 to 0.25
- gain_second: float32 [128], replicated, may hold values from 0.5 to 1.5
- head_weight: bfloat16 [128, 16], replicated, may hold values from -0.5 to 0.5
Outputs:
- query_grad: bfloat16 [16, 512, 768], P('noise', ('qi', 'kj'))
- key_grad: bfloat16 [16, 512, 768], P('noise', ('qi', 'kj'))
- value_grad: bfloat16 [16, 512, 768], P('noise', ('qi', 'kj'))
- pair_grad: bfloat16 [2, 16, 16, 2, 256, 128], P('qi', 'noise', None, None, 'kj')
- gate_grad: float32 [128, 512], replicated
- up_grad: float32 [128, 512], replicated
- down_grad: float32 [512, 128], replicated
- head_grad: float32 [128, 16], replicated
- first_grad: float32 [128], replicated
- second_grad: float32 [128], replicated
The draws below stay inside these ranges and needn't reach their ends.
All inputs are finite; a program needn't handle non-finite values.
Results may differ from the reference program's by a relative error of at most 0.011.
Values may be sent and summed in bfloat16 or wider, within the bound.
No kernel may reach another device: no remote copies, remote signals or barrier semaphores. Data moves between devices by JAX's collectives and lax.ppermute only.
A program may use at most 64 MiB of HBM per device.

```python
import jax
import jax.numpy as jnp
from jax import lax

HEADS = 16
HEAD_DIM = 48
PAIR = 128
FF = 512
WIDTH = 768
TOKENS = 512
QUERY_TILE = 256
ROWS_SUB = 16
COPIES = 16
N_QI = 2


def drawn_draw(key):
    base_key = jax.random.fold_in(key, 4242)
    first_key, second_key = jax.random.split(base_key, 2)
    full_shape = (COPIES, TOKENS, HEADS, HEAD_DIM)
    queries = jnp.clip(jax.random.normal(first_key, full_shape, jnp.float32), -6.0, 6.0)
    keyset = jnp.clip(jax.random.normal(second_key, full_shape, jnp.float32), -6.0, 6.0)
    queries = queries.reshape(COPIES, TOKENS, HEADS * HEAD_DIM)
    keyset = keyset.reshape(COPIES, TOKENS // QUERY_TILE, QUERY_TILE, HEADS * HEAD_DIM)
    return (queries, keyset)


def draw_query_rows(key, part):
    return drawn_draw(key)[0].astype(jnp.bfloat16)


def draw_key_rows(key, part):
    return drawn_draw(key)[1].astype(jnp.bfloat16)


def steps_of(rng, extent, cuts, smallest, high):
    loudness, own = 1.0, jax.random.fold_in(rng, 6)
    for dim, blocks in cuts:
        draws = jnp.exp(jax.random.uniform(jax.random.fold_in(own, dim), (blocks,), jnp.float32, smallest / len(cuts), high / len(cuts)))
        loudness = loudness * jnp.repeat(draws, extent[dim] // blocks).reshape([-1 if axis == dim else 1 for axis in range(len(extent))])
    return loudness


def bell_draw(key, dims, width, limit, shards=(), kind=jnp.bfloat16):
    result = width * jax.random.normal(key, dims, jnp.float32)
    if shards:
        result = result * steps_of(key, dims, shards, -0.22, 0.18)
    return jnp.clip(result, -limit, limit).astype(kind)


def setup_inputs(seed: int = 0) -> dict:
    streams_of = jax.random.split(jax.random.key(seed), 12)
    return {
        "pair_rep": bell_draw(streams_of[0], (TOKENS, N_QI, QUERY_TILE, PAIR), 1.0, 6.0, ((0, 2), (2, 8))),
        "query_rows": draw_query_rows(jax.random.fold_in(streams_of[11], 71), 0),
        "key_rows": draw_key_rows(jax.random.fold_in(streams_of[11], 71), 0),
        "value_rows": bell_draw(streams_of[3], (COPIES, N_QI, QUERY_TILE, WIDTH), 1.0, 6.0, ((0, 16), (2, 8))),
        "output_grad": bell_draw(streams_of[4], (COPIES, TOKENS, WIDTH), (TOKENS / 32), 96.0, ((0, 16), (1, 2))),
        "gain_first": jnp.clip(1.0 + 0.1 * jax.random.normal(streams_of[5], (PAIR,), jnp.float32), 0.5, 1.5),
        "gate_weight": bell_draw(streams_of[6], (PAIR, FF), PAIR ** -0.5, 0.5),
        "up_weight": bell_draw(streams_of[7], (PAIR, FF), PAIR ** -0.5, 0.5),
        "down_weight": bell_draw(streams_of[8], (FF, PAIR), FF ** -0.5, 0.25),
        "gain_second": jnp.clip(1.0 + 0.1 * jax.random.normal(streams_of[9], (PAIR,), jnp.float32), 0.5, 1.5),
        "head_weight": bell_draw(streams_of[10], (PAIR, HEADS), PAIR ** -0.5, 0.5),
    }


epsilon = 1e-05

def layer_norm(values, gain_vec):
    center = values - lax.optimization_barrier(jnp.mean(values, axis=1, keepdims=True))
    inverse = lax.rsqrt(lax.optimization_barrier(jnp.mean(center * center, axis=1, keepdims=True)) + epsilon)
    normed = center * inverse
    return (normed, inverse, normed * gain_vec)

def norm_backward(normed_grad, normed, inverse):
    first_mean = lax.optimization_barrier(jnp.mean(normed_grad, axis=1, keepdims=True))
    second_mean = lax.optimization_barrier(jnp.mean(normed_grad * normed, axis=1, keepdims=True))
    return inverse * (normed_grad - first_mean - normed * second_mean)

def wide_einsum(form, left, right):
    return jnp.einsum(form, left.astype(jnp.float32), right.astype(jnp.float32))

def transition_forward(cells, params):
    gain_first, gate_weight, up_weight, down_weight, gain_second, head_weight = params
    inputs = cells.astype(jnp.float32)
    pre_normed, pre_inverse, pre_scaled = layer_norm(inputs, gain_first)
    pre_lowered = pre_scaled.astype(jnp.bfloat16)
    gate_pre = jnp.dot(pre_lowered, gate_weight, preferred_element_type=jnp.float32)
    up_pre = jnp.dot(pre_lowered, up_weight, preferred_element_type=jnp.float32)
    gate_sigmoid = jax.nn.sigmoid(gate_pre)
    hidden = (gate_pre * gate_sigmoid * up_pre).astype(jnp.bfloat16)
    updated = inputs + jnp.dot(hidden, down_weight, preferred_element_type=jnp.float32)
    post_normed, post_inverse, post_scaled = layer_norm(updated, gain_second)
    post_lowered = post_scaled.astype(jnp.bfloat16)
    bias_heads = wide_einsum('mc,ch->hm', post_lowered, head_weight).astype(jnp.bfloat16)
    saved_state = (pre_normed, pre_inverse, pre_lowered, gate_pre, up_pre, gate_sigmoid, hidden, post_normed, post_inverse, post_lowered)
    return (bias_heads, saved_state)

def transition_backward(saved_state, grad_heads, params):
    gain_first, gate_weight, up_weight, down_weight, gain_second, head_weight = params
    pre_normed, pre_inverse, pre_lowered, gate_pre, up_pre, gate_sigmoid, hidden, post_normed, post_inverse, post_lowered = saved_state
    grad_low = grad_heads.astype(jnp.bfloat16)
    post_scaled = wide_einsum('hm,ch->mc', grad_low, head_weight)
    head_part = wide_einsum('mc,hm->ch', post_lowered, grad_low)
    second_part = lax.optimization_barrier(jnp.sum(post_scaled * post_normed, axis=0))
    updated_grad = norm_backward(post_scaled * gain_second, post_normed, post_inverse)
    updated_low = updated_grad.astype(jnp.bfloat16)
    down_part = wide_einsum('mf,mc->fc', hidden, updated_low)
    hidden_grad = wide_einsum('mc,fc->mf', updated_low, down_weight)
    gate_low = (hidden_grad * up_pre * gate_sigmoid * (1.0 + gate_pre * (1.0 - gate_sigmoid))).astype(jnp.bfloat16)
    up_low = (hidden_grad * gate_pre * gate_sigmoid).astype(jnp.bfloat16)
    gate_part = wide_einsum('mc,mf->cf', pre_lowered, gate_low)
    up_part = wide_einsum('mc,mf->cf', pre_lowered, up_low)
    pre_scaled = wide_einsum('mf,cf->mc', gate_low, gate_weight) + wide_einsum('mf,cf->mc', up_low, up_weight)
    first_part = lax.optimization_barrier(jnp.sum(pre_scaled * pre_normed, axis=0))
    inputs_grad = norm_backward(pre_scaled * gain_first, pre_normed, pre_inverse)
    pair_low = (updated_grad + inputs_grad).astype(jnp.bfloat16)
    return (pair_low, (gate_part, up_part, down_part, head_part, first_part, second_part))

def reference(pair_rep, query_rows, key_rows, value_rows, output_grad, gain_first, gate_weight, up_weight, down_weight, gain_second, head_weight):
    params = (gain_first, gate_weight, up_weight, down_weight, gain_second, head_weight)
    score_scale = HEAD_DIM ** (-0.5)
    block_count = TOKENS // ROWS_SUB
    pair_full = pair_rep.reshape(block_count, ROWS_SUB * TOKENS, PAIR)
    bias_blocks = lax.map(lambda cells: transition_forward(cells, params)[0], pair_full)
    bias_full = bias_blocks.reshape(block_count, HEADS, ROWS_SUB, TOKENS).transpose(1, 0, 2, 3).reshape(HEADS, TOKENS, TOKENS)
    keys_all = key_rows.reshape(COPIES, TOKENS, WIDTH)
    values_all = value_rows.reshape(COPIES, TOKENS, WIDTH)

    def one_copy(running, items):
        query_copy, key_copy, value_copy, grad_copy = items
        query_tile = query_copy.astype(jnp.float32).reshape(TOKENS, HEADS, HEAD_DIM)
        keys_tile = key_copy.astype(jnp.float32).reshape(TOKENS, HEADS, HEAD_DIM)
        values_tile = value_copy.astype(jnp.float32).reshape(TOKENS, HEADS, HEAD_DIM)
        grad_tile = grad_copy.astype(jnp.float32).reshape(TOKENS, HEADS, HEAD_DIM)
        scores = jnp.einsum('qhd,khd->hqk', query_tile, keys_tile) * score_scale + bias_full.astype(jnp.float32)
        largest = lax.optimization_barrier(jnp.max(scores, axis=2, keepdims=True))
        expo = jnp.exp(scores - largest)
        attend = expo / lax.optimization_barrier(jnp.sum(expo, axis=2, keepdims=True))
        attend_grad = jnp.einsum('qhd,khd->hqk', grad_tile, values_tile)
        delta = lax.optimization_barrier(jnp.sum(attend * attend_grad, axis=2, keepdims=True))
        score_grad = attend * (attend_grad - delta)
        score_low = score_grad.astype(jnp.bfloat16).astype(jnp.float32)
        attend_low = attend.astype(jnp.bfloat16).astype(jnp.float32)
        query_out = (jnp.einsum('hqk,khd->qhd', score_low, keys_tile) * score_scale).astype(jnp.bfloat16)
        key_out = (jnp.einsum('hqk,qhd->khd', score_low, query_tile) * score_scale).astype(jnp.bfloat16)
        value_out = jnp.einsum('hqk,qhd->khd', attend_low, grad_tile).astype(jnp.bfloat16)
        return (running + score_grad, (query_out.reshape(TOKENS, WIDTH), key_out.reshape(TOKENS, WIDTH), value_out.reshape(TOKENS, WIDTH)))
    initial = jnp.zeros((HEADS, TOKENS, TOKENS), jnp.float32)
    bias_sum, outputs = lax.scan(one_copy, initial, (query_rows, keys_all, values_all, output_grad))
    query_grad, key_grad, value_grad = outputs
    grad_blocks = bias_sum.reshape(HEADS, block_count, ROWS_SUB * TOKENS).transpose(1, 0, 2)

    def one_block(running, items):
        cells, grad_heads = items
        saved_state = transition_forward(cells, params)[1]
        pair_low, weight_parts = transition_backward(saved_state, grad_heads, params)
        return (tuple((total + part for total, part in zip(running, weight_parts))), pair_low)
    zeros_init = (jnp.zeros((PAIR, FF), jnp.float32), jnp.zeros((PAIR, FF), jnp.float32), jnp.zeros((FF, PAIR), jnp.float32), jnp.zeros((PAIR, HEADS), jnp.float32), jnp.zeros((PAIR,), jnp.float32), jnp.zeros((PAIR,), jnp.float32))
    reduced, pair_blocks = lax.scan(one_block, zeros_init, (pair_full, grad_blocks))
    pair_grad = pair_blocks.reshape(N_QI, COPIES, ROWS_SUB, N_QI, QUERY_TILE, PAIR)
    factor = 1.0 / TOKENS
    return (query_grad, key_grad, value_grad, pair_grad, reduced[0] * factor, reduced[1] * factor, reduced[2] * factor, reduced[3] * factor, reduced[4] * factor, reduced[5] * factor)
```

```python
import functools

import jax
import jax.numpy as jnp
from jax import lax
from jax.experimental import pallas as pl
from jax.experimental.pallas import tpu as pltpu
from jax.sharding import Mesh, PartitionSpec as P

HEADS = 16
HEAD_DIM = 48
WIDTH = HEADS * HEAD_DIM
PAIR = 128
FF = 512
KEYS = 64
ROWS = 256
SUB = 16
EPSILON = 1e-05
SCALE = HEAD_DIM**-0.5
CHUNK_ROWS = 56
CHUNKS = 32
F32 = jnp.float32
BF16 = jnp.bfloat16
NOISE = ("zl", "x")
PLANE = ("x", "qi", "y")
COLUMN = ("zh", "zl")

VMEM = pl.BlockSpec(memory_space=pltpu.VMEM)
SMEM = pl.BlockSpec(memory_space=pltpu.SMEM)
PARAMS = pltpu.CompilerParams(vmem_limit_bytes=48 * 1024 * 1024)


def dot(left, right, dims):
    return lax.dot_general(left, right, (dims, ((), ())), preferred_element_type=F32)


NN = ((1,), (0,))
NT = ((1,), (1,))
TN = ((0,), (0,))


def layer_norm(values):
    center = values - jnp.mean(values, axis=1, keepdims=True)
    inverse = lax.rsqrt(jnp.mean(center * center, axis=1, keepdims=True) + EPSILON)
    return center * inverse, inverse


def norm_backward(grad, normed, inverse):
    first = jnp.mean(grad, axis=1, keepdims=True)
    second = jnp.mean(grad * normed, axis=1, keepdims=True)
    return inverse * (grad - first - normed * second)


def chunk_cells(read_row, chunk):
    slabs = [
        read_row(half * 8 + 2 * chunk + step) for step in range(2) for half in range(2)
    ]
    return jnp.concatenate(slabs, axis=0)


def bias_kernel(place, pair, gain1, gate_w, up_w, down_w, gain2, head_t, out, rows):
    for chunk in range(4):
        cells = chunk_cells(lambda r: pair[r].reshape(KEYS, PAIR), chunk).astype(F32)
        normed, _ = layer_norm(cells)
        lowered = (normed * gain1[...]).astype(BF16)
        gate = dot(lowered, gate_w[...], NN)
        up = dot(lowered, up_w[...], NN)
        hidden = (gate * jax.nn.sigmoid(gate) * up).astype(BF16)
        updated = cells + dot(hidden, down_w[...], NN)
        post, _ = layer_norm(updated)
        post_low = (post * gain2[...]).astype(BF16)
        bias = dot(head_t[...], post_low, NT)
        rows[pl.ds(2 * chunk, HEADS, stride=8), :] = bias[:, :128]
        rows[pl.ds(2 * chunk + 1, HEADS, stride=8), :] = bias[:, 128:]
    out[0] = rows[...].astype(BF16)


def head_mask(shape, head):
    column = lax.broadcasted_iota(jnp.int32, shape, 1)
    return (column >= head * HEAD_DIM) & (column < (head + 1) * HEAD_DIM)


def spread_heads(tile):
    wide = tile.astype(F32)
    parts = [
        jnp.where(head_mask(wide.shape, h), wide, 0.0).astype(BF16) for h in range(HEADS)
    ]
    return jnp.concatenate(parts, axis=0)


def permute_rows(tile):
    width = tile.shape[1]
    wide = tile.astype(F32).reshape(16, 2, 8, width)
    parts = [wide[:, half].reshape(128, width) for half in range(2)]
    return jnp.concatenate(parts, axis=0).astype(BF16)


def product_kernel(query, grad, keys, values, scores, attend, query_out, grad_out, keys_out):
    query_p = permute_rows(query[...])
    grad_p = permute_rows(grad[...])
    query_out[...] = query_p
    grad_out[...] = grad_p
    wide_keys = spread_heads(keys[...].reshape(KEYS, WIDTH))
    keys_out[...] = wide_keys
    scores[...] = dot(wide_keys, query_p, NT) * SCALE
    wide_values = spread_heads(values[...].reshape(KEYS, WIDTH))
    attend[...] = dot(wide_values, grad_p, NT)


def stats_kernel(place, scores, attend, own, first, second, third, expo, stats, wide):
    x = place[1]
    for shift, piece in enumerate((own, first, second, third)):
        origin = lax.rem(x + 4 - shift, 4)
        for zl in range(4):
            wide[zl, origin] = piece[zl].astype(F32)
    for h in range(HEADS):
        block = wide[:, :, 8 * h : 8 * h + 8, :].reshape(128, 128).T
        bias = jnp.concatenate([block[:KEYS], block[KEYS:]], axis=1)
        rows = slice(h * KEYS, (h + 1) * KEYS)
        total = scores[rows, :] + bias
        largest = jnp.max(total, axis=0, keepdims=True)
        powers = jnp.exp(total - largest)
        expo[rows, :] = powers
        stats[h : h + 1, :] = largest
        stats[HEADS + h : HEADS + h + 1, :] = jnp.sum(powers, axis=0, keepdims=True)
        stats[2 * HEADS + h : 2 * HEADS + h + 1, :] = jnp.sum(
            powers * attend[rows, :], axis=0, keepdims=True
        )


def grad_kernel(stats, gathered, expo, attend, send, score_low, attend_low):
    peers = [gathered[j] for j in range(8)]
    largest = functools.reduce(jnp.maximum, [p[:HEADS] for p in peers])
    total = jnp.zeros((HEADS, ROWS), F32)
    weighted = jnp.zeros((HEADS, ROWS), F32)
    for p in peers:
        factor = jnp.exp(p[:HEADS] - largest)
        total = total + p[HEADS : 2 * HEADS] * factor
        weighted = weighted + p[2 * HEADS :] * factor
    factor = jnp.exp(stats[:HEADS, :] - largest) / total
    delta = weighted / total
    for pair in range(HEADS // 2):
        blocks = []
        for h in (2 * pair, 2 * pair + 1):
            rows = slice(h * KEYS, (h + 1) * KEYS)
            weights = expo[rows, :] * factor[h : h + 1]
            score = weights * (attend[rows, :] - delta[h : h + 1])
            score_low[rows, :] = score.astype(BF16)
            attend_low[rows, :] = weights.astype(BF16)
            block = jnp.concatenate([score[:, :128], score[:, 128:]], axis=0).T
            blocks.append(block.reshape(16, 8, 128))
        send[:, 16 * pair : 16 * pair + 16, :] = jnp.concatenate(blocks, axis=1).astype(BF16)


def rows_kernel(place, score_low, attend_low, query, grad, keys, query_send, kv_send):
    y, zh, qi = place[2], place[3], place[4]
    product = dot(score_low[...], keys[...], TN) * SCALE
    for target in range(8):
        rel_z = lax.rem(target // 4 + zh, 2)
        rel_y = lax.rem(target % 4 + 4 - y, 4)
        parts = []
        for block in (2 * target, 2 * target + 1):
            for half in range(2):
                start = half * 128 + block * 8
                parts.append(product[start : start + 8])
        query_send[rel_z, rel_y] = jnp.concatenate(parts, axis=0).astype(BF16)
    for which, (low, rows) in enumerate(((score_low, query), (attend_low, grad))):
        result = jnp.zeros((KEYS, WIDTH), F32)
        for quad in range(4):
            part = dot(low[quad * 256 : quad * 256 + 256, :], rows[...], NN)
            for step in range(4):
                piece = part[step * KEYS : (step + 1) * KEYS]
                mask = head_mask(piece.shape, quad * 4 + step)
                result = result + jnp.where(mask, piece, 0.0)
        if which == 0:
            result = result * SCALE
        for a in range(2):
            rel = lax.rem(a + qi, 2)
            kv_send[rel, :, which * WIDTH : (which + 1) * WIDTH] = result[a * 32 : a * 32 + 32]


def pair_kernel(
    place, pair, received, gain1, gate_w, up_w, down_w, gain2, head_t, pair_out, weights,
    rows, pre_s, gate_s, up_s, hidden_s, updated_s, post_s, low_s,
):
    rows[...] = jnp.sum(received[...].astype(F32), axis=0)
    first_sum = jnp.zeros((1, PAIR), F32)
    second_sum = jnp.zeros((1, PAIR), F32)
    for chunk in range(4):
        span = slice(chunk * 256, (chunk + 1) * 256)
        cells = chunk_cells(lambda r: pair[r].reshape(KEYS, PAIR), chunk).astype(F32)
        pre_normed, pre_inverse = layer_norm(cells)
        lowered = (pre_normed * gain1[...]).astype(BF16)
        pre_s[span, :] = lowered
        gate = dot(lowered, gate_w[...], NN)
        up = dot(lowered, up_w[...], NN)
        sigmoid = jax.nn.sigmoid(gate)
        silu = gate * sigmoid
        hidden = (silu * up).astype(BF16)
        hidden_s[span, :] = hidden
        updated = cells + dot(hidden, down_w[...], NN)
        post_normed, post_inverse = layer_norm(updated)
        post_s[span, :] = (post_normed * gain2[...]).astype(BF16)
        low = jnp.concatenate(
            [rows[pl.ds(2 * chunk + step, HEADS, stride=8), :] for step in range(2)], axis=1
        ).astype(BF16)
        low_s[:, span] = low
        post_scaled = dot(low, head_t[...], TN)
        second_sum = second_sum + jnp.sum(post_scaled * post_normed, axis=0, keepdims=True)
        updated_grad = norm_backward(post_scaled * gain2[...], post_normed, post_inverse)
        updated_low = updated_grad.astype(BF16)
        updated_s[span, :] = updated_low
        hidden_grad = dot(updated_low, down_w[...], NT)
        gate_low = (hidden_grad * up * sigmoid * (1.0 + gate * (1.0 - sigmoid))).astype(BF16)
        up_low = (hidden_grad * silu).astype(BF16)
        gate_s[span, :] = gate_low
        up_s[span, :] = up_low
        pre_scaled = dot(gate_low, gate_w[...], NT) + dot(up_low, up_w[...], NT)
        first_sum = first_sum + jnp.sum(pre_scaled * pre_normed, axis=0, keepdims=True)
        inputs_grad = norm_backward(pre_scaled * gain1[...], pre_normed, pre_inverse)
        result = (updated_grad + inputs_grad).astype(BF16)
        for step in range(2):
            for half in range(2):
                start = step * 128 + half * KEYS
                slab = result[start : start + KEYS]
                pair_out[half * 8 + 2 * chunk + step] = slab.reshape(2, 32, PAIR)
    gate_part = dot(pre_s[...], gate_s[...], TN).astype(BF16)
    up_part = dot(pre_s[...], up_s[...], TN).astype(BF16)
    for block in range(4):
        lanes = slice(block * 128, (block + 1) * 128)
        weights[block * 128 : (block + 1) * 128, :] = gate_part[:, lanes]
        weights[512 + block * 128 : 512 + (block + 1) * 128, :] = up_part[:, lanes]
    weights[1024:1536, :] = dot(hidden_s[...], updated_s[...], TN).astype(BF16)
    weights[1536:1552, :] = dot(low_s[...], post_s[...], NN).astype(BF16)
    gains = jnp.concatenate([first_sum, second_sum, jnp.zeros((14, PAIR), F32)], axis=0)
    weights[1552:1568, :] = gains.astype(BF16)
    weights[1568:, :] = jnp.zeros((CHUNK_ROWS * CHUNKS - 1568, PAIR), BF16)


def shifted(value, axis, shift):
    size = lax.axis_size(axis)
    return lax.ppermute(value, axis, [(i, (i + shift) % size) for i in range(size)])


def all_to_all(value, axes):
    return lax.all_to_all(value, axes, 0, 0, tiled=True)


def local(
    pair_rep, query_rows, key_rows, value_rows, output_grad,
    gain_first, gate_weight, up_weight, down_weight, gain_second, head_weight,
):
    x, zl = lax.axis_index("x"), lax.axis_index("zl")
    y, zh, qi = lax.axis_index("y"), lax.axis_index("zh"), lax.axis_index("qi")
    place = jnp.stack([zl * 4 + x, x, y, zh, qi]).astype(jnp.int32)
    params = (
        gain_first[None], gate_weight, up_weight, down_weight, gain_second[None], head_weight.T,
    )

    def shape(dims, dtype):
        return jax.ShapeDtypeStruct(dims, dtype)

    def whole(array):
        return pl.BlockSpec(array.shape, lambda i, p: (0,) * array.ndim)

    own = pl.pallas_call(
        bias_kernel,
        grid_spec=pltpu.PrefetchScalarGridSpec(
            num_scalar_prefetch=1,
            grid=(4,),
            in_specs=[
                pl.BlockSpec((SUB, 2, 32, PAIR), lambda i, p: (i * 4 + p[1], 0, 0, 0)),
                *[whole(a) for a in params],
            ],
            out_specs=pl.BlockSpec((1, 128, 128), lambda i, p: (i, 0, 0)),
            scratch_shapes=[pltpu.VMEM((128, 128), F32)],
        ),
        out_shape=shape((4, 128, 128), BF16),
        compiler_params=PARAMS,
        name="pair_bias",
    )(place, pair_rep, *params)
    pieces = [shifted(own, "x", s) for s in (1, 2, 3)]

    big = shape((HEADS * KEYS, ROWS), F32)
    small = shape((HEADS * KEYS, ROWS), BF16)
    flat = shape((ROWS, WIDTH), BF16)
    scores, attend, query_p, grad_p, wide_keys = pl.pallas_call(
        product_kernel,
        in_specs=[VMEM] * 4,
        out_specs=[VMEM] * 5,
        out_shape=[big, big, flat, flat, shape((HEADS * KEYS, WIDTH), BF16)],
        compiler_params=PARAMS,
        name="products",
    )(query_rows[0], output_grad[0], key_rows[0], value_rows[0])

    expo, stats = pl.pallas_call(
        stats_kernel,
        in_specs=[SMEM] + [VMEM] * 6,
        out_specs=[VMEM] * 2,
        out_shape=[big, shape((3 * HEADS, ROWS), F32)],
        scratch_shapes=[pltpu.VMEM((4, 4, 128, 128), F32)],
        compiler_params=PARAMS,
        name="softmax_stats",
    )(place, scores, attend, own, *pieces)

    gathered = all_to_all(jnp.broadcast_to(stats[None], (8, *stats.shape)), ("zh", "y"))

    send, score_low, attend_low = pl.pallas_call(
        grad_kernel,
        in_specs=[VMEM] * 4,
        out_specs=[VMEM] * 3,
        out_shape=[shape((16, 128, 128), BF16), small, small],
        compiler_params=PARAMS,
        name="score_grads",
    )(stats, gathered, expo, attend)

    received = all_to_all(send, NOISE)

    query_send, kv_send = pl.pallas_call(
        rows_kernel,
        in_specs=[SMEM] + [VMEM] * 5,
        out_specs=[VMEM] * 2,
        out_shape=[shape((2, 4, 32, WIDTH), BF16), shape((2, 32, 2 * WIDTH), F32)],
        compiler_params=PARAMS,
        name="row_grads",
    )(place, score_low, attend_low, query_p, grad_p, wide_keys)

    half = query_send[0].astype(F32) + shifted(query_send[1], "zh", 1).astype(F32)
    quarter = half.astype(BF16)
    query_sum = half[0]
    for s in (1, 2, 3):
        query_sum = query_sum + shifted(quarter[s], "y", s).astype(F32)
    query_grad = query_sum.astype(BF16)[None]
    kv_sum = (kv_send[0] + shifted(kv_send[1], "qi", 1)).astype(BF16)
    key_grad = kv_sum[None, :, :WIDTH]
    value_grad = kv_sum[None, :, WIDTH:]

    weight_rows = CHUNK_ROWS * CHUNKS
    pair_low, weights = pl.pallas_call(
        pair_kernel,
        grid_spec=pltpu.PrefetchScalarGridSpec(
            num_scalar_prefetch=1,
            grid=(1,),
            in_specs=[
                pl.BlockSpec((SUB, 2, 32, PAIR), lambda i, p: (p[0], 0, 0, 0)),
                whole(received),
                *[whole(a) for a in params],
            ],
            out_specs=[
                pl.BlockSpec((SUB, 2, 32, PAIR), lambda i, p: (0, 0, 0, 0)),
                pl.BlockSpec((weight_rows, PAIR), lambda i, p: (0, 0)),
            ],
            scratch_shapes=[
                pltpu.VMEM((128, 128), F32),
                pltpu.VMEM((1024, PAIR), BF16),
                pltpu.VMEM((1024, FF), BF16),
                pltpu.VMEM((1024, FF), BF16),
                pltpu.VMEM((1024, FF), BF16),
                pltpu.VMEM((1024, PAIR), BF16),
                pltpu.VMEM((1024, PAIR), BF16),
                pltpu.VMEM((HEADS, 1024), BF16),
            ],
        ),
        out_shape=[shape((SUB, 2, 32, PAIR), BF16), shape((weight_rows, PAIR), BF16)],
        compiler_params=PARAMS,
        name="pair_backward",
    )(place, pair_rep, received, *params)
    pair_grad = pair_low[None, None]

    parts = all_to_all(weights.reshape(CHUNKS, CHUNK_ROWS, PAIR), PLANE)
    share = jnp.sum(parts.astype(F32), axis=0).astype(BF16)
    columns = all_to_all(jnp.broadcast_to(share[None], (8, *share.shape)), COLUMN)
    total = jnp.sum(columns.astype(F32), axis=0).astype(BF16)
    everything = all_to_all(jnp.broadcast_to(total[None], (CHUNKS, *total.shape)), PLANE)
    factor = 1.0 / 512
    table = everything.reshape(weight_rows, PAIR).astype(F32) * factor

    def wide_rows(start):
        block = table[start : start + 512].reshape(4, 128, 128)
        return block.transpose(1, 0, 2).reshape(PAIR, FF)

    return (
        query_grad,
        key_grad,
        value_grad,
        pair_grad,
        wide_rows(0),
        wide_rows(512),
        table[1024:1536],
        table[1536:1552].T,
        table[1552],
        table[1553],
    )


def solution(mesh):
    fine = Mesh(mesh.devices.reshape(4, 4, 2, 2, 4), ("zl", "x", "qi", "zh", "y"))
    kj = ("zh", "y")
    return jax.shard_map(
        local,
        mesh=fine,
        in_specs=(
            P("qi", None, kj, None),
            P(NOISE, "qi", None),
            P(NOISE, None, kj, None),
            P(NOISE, None, kj, None),
            P(NOISE, "qi", None),
            P(),
            P(),
            P(),
            P(),
            P(),
            P(),
        ),
        out_specs=(
            P(NOISE, ("qi", "zh", "y"), None),
            P(NOISE, ("qi", "zh", "y"), None),
            P(NOISE, ("qi", "zh", "y"), None),
            P("qi", NOISE, None, None, kj, None),
            P(),
            P(),
            P(),
            P(),
            P(),
            P(),
        ),
        check_vma=False,
    )
```

```python
import functools

import jax
import jax.numpy as jnp
from jax import lax
from jax.experimental import pallas as pl
from jax.experimental.pallas import tpu as pltpu
from jax.sharding import Mesh, PartitionSpec as P

HEADS = 16
HEAD_DIM = 48
WIDTH = HEADS * HEAD_DIM
PAIR = 128
FF = 512
KEYS = 64
ROWS = 256
SUB = 16
EPSILON = 1e-05
SCALE = HEAD_DIM**-0.5
CHUNK_ROWS = 56
CHUNKS = 32
GROUP = 4
F32 = jnp.float32
BF16 = jnp.bfloat16
NOISE = ("zl", "x")
PLANE = ("x", "qi", "y")
COLUMN = ("zh", "zl")

VMEM = pl.BlockSpec(memory_space=pltpu.VMEM)
SMEM = pl.BlockSpec(memory_space=pltpu.SMEM)
HBM = pl.BlockSpec(memory_space=pltpu.HBM)
BLOCK = pl.BlockSpec()
PARAMS = pltpu.CompilerParams(vmem_limit_bytes=48 * 1024 * 1024)


def dot(left, right, dims):
    return lax.dot_general(left, right, (dims, ((), ())), preferred_element_type=F32)


NN = ((1,), (0,))
NT = ((1,), (1,))
TN = ((0,), (0,))


def layer_norm(values):
    center = values - jnp.mean(values, axis=1, keepdims=True)
    inverse = lax.rsqrt(jnp.mean(center * center, axis=1, keepdims=True) + EPSILON)
    return center * inverse, inverse


def norm_backward(grad, normed, inverse):
    first = jnp.mean(grad, axis=1, keepdims=True)
    second = jnp.mean(grad * normed, axis=1, keepdims=True)
    return inverse * (grad - first - normed * second)


def block_cells(read_row):
    slabs = [read_row(half * 8 + step) for step in range(8) for half in range(2)]
    return jnp.concatenate(slabs, axis=0)


def silu_parts(gate):
    half = 0.5 * gate
    curve = jnp.tanh(half)
    return half + half * curve, 0.5 + 0.5 * curve


def fetch(sources, targets, sems):
    copies = [
        pltpu.make_async_copy(source, target, sems.at[k])
        for k, (source, target) in enumerate(zip(sources, targets))
    ]
    for copy in copies:
        copy.start()
    return copies


def bias_kernel(
    place, pair, gain1_h, gate_h, up_h, down_h, gain2_h, head_h, out,
    cells_v, gain1, gate_w, up_w, down_w, gain2, head_t, rows, sems,
):
    x = place[1]
    blocks = [pair.at[pl.ds((zl * 4 + x) * SUB, SUB)] for zl in range(4)]
    copies = fetch(
        (blocks[0], gain1_h, gate_h, up_h, down_h, gain2_h, head_h, *blocks[1:]),
        (
            cells_v.at[0], gain1, gate_w, up_w, down_w, gain2, head_t,
            cells_v.at[1], cells_v.at[2], cells_v.at[3],
        ),
        sems,
    )
    for copy in copies:
        copy.wait()
    for start in range(0, 4, GROUP):
        blocks = range(start, start + GROUP)
        cells = jnp.concatenate(
            [block_cells(lambda r: cells_v[k, r].reshape(KEYS, PAIR)) for k in blocks], axis=0
        ).astype(F32)
        normed, _ = layer_norm(cells)
        lowered = (normed * gain1[...]).astype(BF16)
        gate = dot(lowered, gate_w[...], NN)
        up = dot(lowered, up_w[...], NN)
        hidden = (silu_parts(gate)[0] * up).astype(BF16)
        updated = cells + dot(hidden, down_w[...], NN)
        post, _ = layer_norm(updated)
        post_low = (post * gain2[...]).astype(BF16)
        bias = dot(head_t[...], post_low, NT)
        for place_k, k in enumerate(blocks):
            for step in range(8):
                lane = place_k * 1024 + step * 128
                rows[k, pl.ds(step, HEADS, stride=8), :] = bias[:, lane : lane + 128]
            out[k] = rows[k].astype(BF16)


def head_mask(shape, head):
    column = lax.broadcasted_iota(jnp.int32, shape, 1)
    return (column >= head * HEAD_DIM) & (column < (head + 1) * HEAD_DIM)


def spread_heads(tile):
    wide = tile.astype(F32)
    parts = [
        jnp.where(head_mask(wide.shape, h), wide, 0.0).astype(BF16) for h in range(HEADS)
    ]
    return jnp.concatenate(parts, axis=0)


def permute_rows(tile):
    width = tile.shape[1]
    wide = tile.astype(F32).reshape(16, 2, 8, width)
    parts = [wide[:, half].reshape(128, width) for half in range(2)]
    return jnp.concatenate(parts, axis=0).astype(BF16)


def product_kernel(query, grad, keys, values, scores, attend, query_out, grad_out, keys_out):
    query_p = permute_rows(query[...])
    grad_p = permute_rows(grad[...])
    query_out[...] = query_p
    grad_out[...] = grad_p
    wide_keys = spread_heads(keys[...].reshape(KEYS, WIDTH))
    keys_out[...] = wide_keys
    scores[...] = dot(wide_keys, query_p, NT) * SCALE
    wide_values = spread_heads(values[...].reshape(KEYS, WIDTH))
    attend[...] = dot(wide_values, grad_p, NT)


def stats_kernel(place, scores, attend, own, first, second, third, total_out, stats, wide):
    x = place[1]
    for shift, piece in enumerate((own, first, second, third)):
        origin = lax.rem(x + 4 - shift, 4)
        for zl in range(4):
            wide[zl, origin] = piece[zl].astype(F32)
    logs, means = [], []
    for h in range(HEADS):
        block = wide[:, :, 8 * h : 8 * h + 8, :].reshape(128, 128).T
        bias = jnp.concatenate([block[:KEYS], block[KEYS:]], axis=1)
        rows = slice(h * KEYS, (h + 1) * KEYS)
        total = scores[rows, :] + bias
        total_out[rows, :] = total
        largest = jnp.max(total, axis=0, keepdims=True)
        powers = jnp.exp(total - largest)
        amount = jnp.sum(powers, axis=0, keepdims=True)
        weighted = jnp.sum(powers * attend[rows, :], axis=0, keepdims=True)
        logs.append(largest + jnp.log(amount))
        means.append(weighted / amount)
    packed = jnp.concatenate(logs + means, axis=0)
    for j in range(8):
        stats[j] = packed


def grad_kernel(gathered, total, attend, send, score_low, attend_low):
    peers = [gathered[j] for j in range(8)]
    largest = functools.reduce(jnp.maximum, [p[:HEADS] for p in peers])
    amount = jnp.zeros((HEADS, ROWS), F32)
    weighted = jnp.zeros((HEADS, ROWS), F32)
    for p in peers:
        power = jnp.exp(p[:HEADS] - largest)
        amount = amount + power
        weighted = weighted + p[HEADS:] * power
    level = largest + jnp.log(amount)
    delta = weighted / amount
    for pair in range(HEADS // 2):
        blocks = []
        for h in (2 * pair, 2 * pair + 1):
            rows = slice(h * KEYS, (h + 1) * KEYS)
            weights = jnp.exp(total[rows, :] - level[h : h + 1])
            score = weights * (attend[rows, :] - delta[h : h + 1])
            score_low[rows, :] = score.astype(BF16)
            attend_low[rows, :] = weights.astype(BF16)
            block = jnp.concatenate([score[:, :128], score[:, 128:]], axis=0).T
            blocks.append(block.reshape(16, 8, 128))
        send[:, 16 * pair : 16 * pair + 16, :] = jnp.concatenate(blocks, axis=1).astype(BF16)


def rows_kernel(
    place, score_low, attend_low, query, grad, keys,
    query_0, query_1, query_2, query_3, kv_keep, kv_send, sends,
):
    y, zh, qi = place[2], place[3], place[4]
    product = dot(score_low[...], keys[...], TN) * SCALE
    for target in range(8):
        rel_z = lax.rem(target // 4 + zh, 2)
        rel_y = lax.rem(target % 4 + 4 - y, 4)
        parts = []
        for block in (2 * target, 2 * target + 1):
            for half in range(2):
                start = half * 128 + block * 8
                parts.append(product[start : start + 8])
        sends[rel_y, rel_z] = jnp.concatenate(parts, axis=0).astype(BF16)
    for shift, out in enumerate((query_0, query_1, query_2, query_3)):
        out[...] = sends[shift]
    for which, (low, rows) in enumerate(((score_low, query), (attend_low, grad))):
        result = jnp.zeros((KEYS, WIDTH), F32)
        for quad in range(4):
            part = dot(low[quad * 256 : quad * 256 + 256, :], rows[...], NN)
            for step in range(4):
                piece = part[step * KEYS : (step + 1) * KEYS]
                mask = head_mask(piece.shape, quad * 4 + step)
                result = result + jnp.where(mask, piece, 0.0)
        if which == 0:
            result = result * SCALE
        lanes = slice(which * WIDTH, (which + 1) * WIDTH)
        first, second = result[:32], result[32:]
        kv_keep[:, lanes] = jnp.where(qi == 0, first, second)
        kv_send[:, lanes] = jnp.where(qi == 0, second, first)


def pair_kernel(
    place, received, pair, gain1, gate_w, up_w, down_w, gain2, head_t,
    pair_out, weights, rows, cells_v, sems,
):
    copies = fetch((pair.at[pl.ds(place[0] * SUB, SUB)],), (cells_v,), sems)
    rows[...] = jnp.sum(received[...].astype(F32), axis=0)
    low = jnp.concatenate(
        [rows[pl.ds(step, HEADS, stride=8), :] for step in range(8)], axis=1
    ).astype(BF16)
    post_scaled = dot(low, head_t[...], TN)
    for copy in copies:
        copy.wait()
    cells = block_cells(lambda r: cells_v[r].reshape(KEYS, PAIR)).astype(F32)
    pre_normed, pre_inverse = layer_norm(cells)
    pre_low = (pre_normed * gain1[...]).astype(BF16)
    gate = dot(pre_low, gate_w[...], NN)
    up = dot(pre_low, up_w[...], NN)
    silu, sigmoid = silu_parts(gate)
    hidden = (silu * up).astype(BF16)
    gate_slope = up * (sigmoid + silu * (1.0 - sigmoid))
    updated = cells + dot(hidden, down_w[...], NN)
    post_normed, post_inverse = layer_norm(updated)
    post_low = (post_normed * gain2[...]).astype(BF16)
    second_sum = jnp.sum(post_scaled * post_normed, axis=0, keepdims=True)
    updated_grad = norm_backward(post_scaled * gain2[...], post_normed, post_inverse)
    updated_low = updated_grad.astype(BF16)
    hidden_grad = dot(updated_low, down_w[...], NT)
    gate_low = (hidden_grad * gate_slope).astype(BF16)
    up_low = (hidden_grad * silu).astype(BF16)
    gate_part = dot(pre_low, gate_low, TN).astype(BF16)
    up_part = dot(pre_low, up_low, TN).astype(BF16)
    for block in range(4):
        lanes = slice(block * 128, (block + 1) * 128)
        weights[block * 128 : (block + 1) * 128, :] = gate_part[:, lanes]
        weights[512 + block * 128 : 512 + (block + 1) * 128, :] = up_part[:, lanes]
    weights[1024:1536, :] = dot(hidden, updated_low, TN).astype(BF16)
    weights[1536:1552, :] = dot(low, post_low, NN).astype(BF16)
    pre_scaled = dot(gate_low, gate_w[...], NT) + dot(up_low, up_w[...], NT)
    first_sum = jnp.sum(pre_scaled * pre_normed, axis=0, keepdims=True)
    inputs_grad = norm_backward(pre_scaled * gain1[...], pre_normed, pre_inverse)
    result = (updated_grad + inputs_grad).astype(BF16)
    for step in range(8):
        for half in range(2):
            start = step * 128 + half * KEYS
            slab = result[start : start + KEYS]
            pair_out[half * 8 + step] = slab.reshape(2, 32, PAIR)
    gains = jnp.concatenate([first_sum, second_sum, jnp.zeros((14, PAIR), F32)], axis=0)
    weights[1552:1568, :] = gains.astype(BF16)
    weights[1568:, :] = jnp.zeros((CHUNK_ROWS * CHUNKS - 1568, PAIR), BF16)


def sum_kernel(parts, out):
    total = jnp.sum(parts[...].astype(F32), axis=0).astype(out.dtype)
    for j in range(out.shape[0]):
        out[j] = total


def unpack_kernel(table, gate_out, up_out, down_out, head_out, first_out, second_out):
    factor = 1.0 / 512
    for block in range(4):
        lanes = slice(block * 128, (block + 1) * 128)
        rows = slice(block * 128, (block + 1) * 128)
        later = slice(512 + block * 128, 512 + (block + 1) * 128)
        gate_out[:, lanes] = table[rows, :].astype(F32) * factor
        up_out[:, lanes] = table[later, :].astype(F32) * factor
    down_out[...] = table[1024:1536, :].astype(F32) * factor
    rest = table[1536:1568, :].astype(F32) * factor
    head_out[...] = rest[:16]
    first_out[...] = rest[16:17]
    second_out[...] = rest[17:18]


def shifted(value, axis, shift):
    size = lax.axis_size(axis)
    return lax.ppermute(value, axis, [(i, (i + shift) % size) for i in range(size)])


def all_to_all(value, axes):
    return lax.all_to_all(value, axes, 0, 0, tiled=True)


def local(
    pair_rep, query_rows, key_rows, value_rows, output_grad,
    gain_first, gate_weight, up_weight, down_weight, gain_second, head_weight,
):
    x, zl = lax.axis_index("x"), lax.axis_index("zl")
    y, zh, qi = lax.axis_index("y"), lax.axis_index("zh"), lax.axis_index("qi")
    place = jnp.stack([zl * 4 + x, x, y, zh, qi]).astype(jnp.int32)
    params = (
        gain_first[None], gate_weight, up_weight, down_weight, gain_second[None], head_weight.T,
    )

    def call(kernel, ins, outs, name, scratch=()):
        return pl.pallas_call(
            kernel,
            in_specs=[spec for spec, _ in ins],
            out_specs=[spec for spec, _ in outs],
            out_shape=[out for _, out in outs],
            scratch_shapes=list(scratch),
            compiler_params=PARAMS,
            name=name,
        )(*[value for _, value in ins])

    def vmem(*values):
        return [(VMEM, value) for value in values]

    def kept(*values):
        return [(BLOCK, pltpu.with_memory_space_constraint(v, pltpu.HBM)) for v in values]

    def f32(*dims):
        return (VMEM, jax.ShapeDtypeStruct(dims, F32))

    def bf16(*dims):
        return (VMEM, jax.ShapeDtypeStruct(dims, BF16))

    def f32_kept(*dims):
        return (BLOCK, pltpu.HBM(dims, F32))

    def bf16_kept(*dims):
        return (BLOCK, pltpu.HBM(dims, BF16))

    def in_hbm(value):
        return (HBM, pltpu.with_memory_space_constraint(value, pltpu.HBM))

    (own,) = call(
        bias_kernel,
        [(SMEM, place), in_hbm(pair_rep), *[in_hbm(p) for p in params]],
        [bf16(4, 128, 128)],
        "pair_bias",
        [
            pltpu.VMEM((4, SUB, 2, 32, PAIR), BF16),
            *[pltpu.VMEM(p.shape, p.dtype) for p in params],
            pltpu.VMEM((4, 128, 128), F32),
            pltpu.SemaphoreType.DMA((10,)),
        ],
    )
    first, third, second = [shifted(own, "x", s) for s in (1, 3, 2)]

    scores, attend, query_p, grad_p, wide_keys = call(
        product_kernel,
        vmem(query_rows[0], output_grad[0], key_rows[0], value_rows[0]),
        [
            f32(HEADS * KEYS, ROWS), f32(HEADS * KEYS, ROWS), bf16_kept(ROWS, WIDTH),
            bf16_kept(ROWS, WIDTH), bf16_kept(HEADS * KEYS, WIDTH),
        ],
        "products",
    )

    total, stats = call(
        stats_kernel,
        [(SMEM, place), *vmem(scores, attend, own, first, second, third)],
        [f32(HEADS * KEYS, ROWS), f32_kept(8, 2 * HEADS, ROWS)],
        "softmax_stats",
        [pltpu.VMEM((4, 4, 128, 128), F32)],
    )

    gathered = all_to_all(stats, ("zh", "y"))

    send, score_low, attend_low = call(
        grad_kernel,
        vmem(gathered, total, attend),
        [bf16_kept(16, 128, 128), *[bf16_kept(HEADS * KEYS, ROWS)] * 2],
        "score_grads",
    )

    received = all_to_all(send, NOISE)

    *query_parts, kv_keep, kv_send = call(
        rows_kernel,
        [(SMEM, place), *kept(score_low, attend_low, query_p, grad_p, wide_keys)],
        [*[bf16(2, 32, WIDTH)] * 4, *[f32(32, 2 * WIDTH)] * 2],
        "row_grads",
        [pltpu.VMEM((4, 2, 32, WIDTH), BF16)],
    )

    half = query_parts[0].astype(F32)
    for s in (1, 3, 2):
        half = half + shifted(query_parts[s], "y", s).astype(F32)
    query_sum = half[0] + shifted(half[1].astype(BF16), "zh", 1).astype(F32)
    query_grad = query_sum.astype(BF16)[None]
    kv_sum = (kv_keep + shifted(kv_send, "qi", 1)).astype(BF16)
    key_grad = kv_sum[None, :, :WIDTH]
    value_grad = kv_sum[None, :, WIDTH:]

    weight_rows = CHUNK_ROWS * CHUNKS
    pair_low, weights = call(
        pair_kernel,
        [(SMEM, place), *vmem(received), in_hbm(pair_rep), *vmem(*params)],
        [bf16_kept(SUB, 2, 32, PAIR), bf16_kept(weight_rows, PAIR)],
        "pair_backward",
        [
            pltpu.VMEM((128, 128), F32),
            pltpu.VMEM((SUB, 2, 32, PAIR), BF16),
            pltpu.SemaphoreType.DMA((1,)),
        ],
    )
    pair_grad = pair_low[None, None]

    parts = all_to_all(weights.reshape(CHUNKS, CHUNK_ROWS, PAIR), PLANE)
    (shares,) = call(sum_kernel, vmem(parts), [bf16_kept(8, CHUNK_ROWS, PAIR)], "plane_sum")
    columns = all_to_all(shares, COLUMN)
    (totals,) = call(
        sum_kernel, vmem(columns), [bf16_kept(CHUNKS, CHUNK_ROWS, PAIR)], "column_sum"
    )
    table = all_to_all(totals, PLANE).reshape(weight_rows, PAIR)
    gate_grad, up_grad, down_grad, head_grad, first_grad, second_grad = call(
        unpack_kernel,
        vmem(table),
        [
            f32_kept(PAIR, FF), f32_kept(PAIR, FF), f32_kept(FF, PAIR),
            f32_kept(HEADS, PAIR), f32_kept(1, PAIR), f32_kept(1, PAIR),
        ],
        "unpack",
    )
    return (
        query_grad, key_grad, value_grad, pair_grad, gate_grad, up_grad, down_grad,
        head_grad.T, first_grad[0], second_grad[0],
    )


def solution(mesh):
    fine = Mesh(mesh.devices.reshape(4, 4, 2, 2, 4), ("zl", "x", "qi", "zh", "y"))
    kj = ("zh", "y")
    return jax.shard_map(
        local,
        mesh=fine,
        in_specs=(
            P("qi", None, kj, None),
            P(NOISE, "qi", None),
            P(NOISE, None, kj, None),
            P(NOISE, None, kj, None),
            P(NOISE, "qi", None),
            P(),
            P(),
            P(),
            P(),
            P(),
            P(),
        ),
        out_specs=(
            P(NOISE, ("qi", "zh", "y"), None),
            P(NOISE, ("qi", "zh", "y"), None),
            P(NOISE, ("qi", "zh", "y"), None),
            P("qi", NOISE, None, None, kj, None),
            P(),
            P(),
            P(),
            P(),
            P(),
            P(),
        ),
        check_vma=False,
    )
```

```python
import functools

import jax
import jax.numpy as jnp
from jax import lax
from jax.experimental import pallas as pl
from jax.experimental.pallas import tpu as pltpu
from jax.sharding import Mesh, PartitionSpec as P

HEADS = 16
HEAD_DIM = 48
WIDTH = HEADS * HEAD_DIM
PAIR = 128
FF = 512
KEYS = 64
ROWS = 256
SUB = 16
EPSILON = 1e-05
SCALE = HEAD_DIM**-0.5
CHUNK_ROWS = 56
CHUNKS = 32
GROUP = 4
F32 = jnp.float32
BF16 = jnp.bfloat16
NOISE = ("zl", "x")
PLANE = ("x", "qi", "y")
COLUMN = ("zh", "zl")

VMEM = pl.BlockSpec(memory_space=pltpu.VMEM)
SMEM = pl.BlockSpec(memory_space=pltpu.SMEM)
HBM = pl.BlockSpec(memory_space=pltpu.HBM)
BLOCK = pl.BlockSpec()
PARAMS = pltpu.CompilerParams(vmem_limit_bytes=48 * 1024 * 1024)


def dot(left, right, dims):
    return lax.dot_general(left, right, (dims, ((), ())), preferred_element_type=F32)


NN = ((1,), (0,))
NT = ((1,), (1,))
TN = ((0,), (0,))


def layer_norm(values):
    center = values - jnp.mean(values, axis=1, keepdims=True)
    inverse = lax.rsqrt(jnp.mean(center * center, axis=1, keepdims=True) + EPSILON)
    return center * inverse, inverse


def norm_backward(grad, normed, inverse):
    first = jnp.mean(grad, axis=1, keepdims=True)
    second = jnp.mean(grad * normed, axis=1, keepdims=True)
    return inverse * (grad - first - normed * second)


def block_cells(read_row):
    slabs = [read_row(half * 8 + step) for step in range(8) for half in range(2)]
    return jnp.concatenate(slabs, axis=0)


def silu_parts(gate):
    half = 0.5 * gate
    curve = jnp.tanh(half)
    return half + half * curve, 0.5 + 0.5 * curve


def fetch(sources, targets, sems):
    copies = [
        pltpu.make_async_copy(source, target, sems.at[k])
        for k, (source, target) in enumerate(zip(sources, targets))
    ]
    for copy in copies:
        copy.start()
    return copies


def bias_kernel(
    place, pair, gain1_h, gate_h, up_h, down_h, gain2_h, head_h, out,
    cells_v, gain1, gate_w, up_w, down_w, gain2, head_t, rows, sems,
):
    x = place[1]
    blocks = [pair.at[pl.ds((zl * 4 + x) * SUB, SUB)] for zl in range(4)]
    copies = fetch(
        (blocks[0], gain1_h, gate_h, up_h, down_h, gain2_h, head_h, *blocks[1:]),
        (
            cells_v.at[0], gain1, gate_w, up_w, down_w, gain2, head_t,
            cells_v.at[1], cells_v.at[2], cells_v.at[3],
        ),
        sems,
    )
    for copy in copies:
        copy.wait()
    for start in range(0, 4, GROUP):
        blocks = range(start, start + GROUP)
        cells = jnp.concatenate(
            [block_cells(lambda r: cells_v[k, r].reshape(KEYS, PAIR)) for k in blocks], axis=0
        ).astype(F32)
        normed, _ = layer_norm(cells)
        lowered = (normed * gain1[...]).astype(BF16)
        gate = dot(lowered, gate_w[...], NN)
        up = dot(lowered, up_w[...], NN)
        hidden = (silu_parts(gate)[0] * up).astype(BF16)
        updated = cells + dot(hidden, down_w[...], NN)
        post, _ = layer_norm(updated)
        post_low = (post * gain2[...]).astype(BF16)
        bias = dot(head_t[...], post_low, NT)
        for place_k, k in enumerate(blocks):
            for step in range(8):
                lane = place_k * 1024 + step * 128
                rows[k, pl.ds(step, HEADS, stride=8), :] = bias[:, lane : lane + 128]
            out[k] = rows[k].astype(BF16)


def head_mask(shape, head):
    column = lax.broadcasted_iota(jnp.int32, shape, 1)
    return (column >= head * HEAD_DIM) & (column < (head + 1) * HEAD_DIM)


def spread_heads(tile):
    wide = tile.astype(F32)
    parts = [
        jnp.where(head_mask(wide.shape, h), wide, 0.0).astype(BF16) for h in range(HEADS)
    ]
    return jnp.concatenate(parts, axis=0)


def permute_rows(tile):
    width = tile.shape[1]
    wide = tile.astype(F32).reshape(16, 2, 8, width)
    parts = [wide[:, half].reshape(128, width) for half in range(2)]
    return jnp.concatenate(parts, axis=0).astype(BF16)


def product_kernel(query, grad, keys, values, scores, attend, query_out, grad_out, keys_out):
    query_p = permute_rows(query[...])
    grad_p = permute_rows(grad[...])
    query_out[...] = query_p
    grad_out[...] = grad_p
    wide_keys = spread_heads(keys[...].reshape(KEYS, WIDTH))
    keys_out[...] = wide_keys
    scores[...] = dot(wide_keys, query_p, NT) * SCALE
    wide_values = spread_heads(values[...].reshape(KEYS, WIDTH))
    attend[...] = dot(wide_values, grad_p, NT)


def stats_kernel(place, scores, attend, own, first, second, third, total_out, stats, wide):
    x = place[1]
    for shift, piece in enumerate((own, first, second, third)):
        origin = lax.rem(x + 4 - shift, 4)
        for zl in range(4):
            wide[zl, origin] = piece[zl].astype(F32)
    logs, means = [], []
    for h in range(HEADS):
        block = wide[:, :, 8 * h : 8 * h + 8, :].reshape(128, 128).T
        bias = jnp.concatenate([block[:KEYS], block[KEYS:]], axis=1)
        rows = slice(h * KEYS, (h + 1) * KEYS)
        total = scores[rows, :] + bias
        total_out[rows, :] = total
        largest = jnp.max(total, axis=0, keepdims=True)
        powers = jnp.exp(total - largest)
        amount = jnp.sum(powers, axis=0, keepdims=True)
        weighted = jnp.sum(powers * attend[rows, :], axis=0, keepdims=True)
        logs.append(largest + jnp.log(amount))
        means.append(weighted / amount)
    stats[...] = jnp.concatenate(logs + means, axis=0)


def merge_stats(parts):
    largest = functools.reduce(jnp.maximum, [p[:HEADS] for p in parts])
    powers = [jnp.exp(p[:HEADS] - largest) for p in parts]
    amount = functools.reduce(jnp.add, powers)
    weighted = functools.reduce(jnp.add, [p[HEADS:] * w for p, w in zip(parts, powers)])
    return largest + jnp.log(amount), weighted / amount


def merge_kernel(own, received, after, merged):
    level, delta = merge_stats([own[...], received[...]])
    merged[:HEADS, :] = level
    merged[HEADS:, :] = delta


def grad_kernel(own, first, second, third, total, attend, send, score_low, attend_low):
    level, delta = merge_stats([own[...], first[...], second[...], third[...]])
    for pair in range(HEADS // 2):
        blocks = []
        for h in (2 * pair, 2 * pair + 1):
            rows = slice(h * KEYS, (h + 1) * KEYS)
            weights = jnp.exp(total[rows, :] - level[h : h + 1])
            score = weights * (attend[rows, :] - delta[h : h + 1])
            score_low[rows, :] = score.astype(BF16)
            attend_low[rows, :] = weights.astype(BF16)
            block = jnp.concatenate([score[:, :128], score[:, 128:]], axis=0).T
            blocks.append(block.reshape(16, 8, 128))
        send[:, 16 * pair : 16 * pair + 16, :] = jnp.concatenate(blocks, axis=1).astype(BF16)


def rows_kernel(
    place, score_low, attend_low, query, grad, keys,
    query_0, query_1, query_2, query_3, kv_keep, kv_send, sends,
):
    y, zh, qi = place[2], place[3], place[4]
    product = dot(score_low[...], keys[...], TN) * SCALE
    for target in range(8):
        rel_z = lax.rem(target // 4 + zh, 2)
        rel_y = lax.rem(target % 4 + 4 - y, 4)
        parts = []
        for block in (2 * target, 2 * target + 1):
            for half in range(2):
                start = half * 128 + block * 8
                parts.append(product[start : start + 8])
        sends[rel_y, rel_z] = jnp.concatenate(parts, axis=0).astype(BF16)
    for shift, out in enumerate((query_0, query_1, query_2, query_3)):
        out[...] = sends[shift]
    for which, (low, rows) in enumerate(((score_low, query), (attend_low, grad))):
        result = jnp.zeros((KEYS, WIDTH), F32)
        for quad in range(4):
            part = dot(low[quad * 256 : quad * 256 + 256, :], rows[...], NN)
            for step in range(4):
                piece = part[step * KEYS : (step + 1) * KEYS]
                mask = head_mask(piece.shape, quad * 4 + step)
                result = result + jnp.where(mask, piece, 0.0)
        if which == 0:
            result = result * SCALE
        lanes = slice(which * WIDTH, (which + 1) * WIDTH)
        first, second = result[:32], result[32:]
        kv_keep[:, lanes] = jnp.where(qi == 0, first, second)
        kv_send[:, lanes] = jnp.where(qi == 0, second, first)


def state_kernel(
    place, after, pair, gain1, gate_w, up_w, down_w, gain2, head_t,
    post_normed_s, post_inverse_s, gate_slope, up_slope, pre_t, hidden_s, post_low,
    pre_normed_s, pre_inverse_s, cells_v, sems,
):
    for copy in fetch((pair.at[pl.ds(place[0] * SUB, SUB)],), (cells_v,), sems):
        copy.wait()
    cells = block_cells(lambda r: cells_v[r].reshape(KEYS, PAIR)).astype(F32)
    normed, inverse = layer_norm(cells)
    pre_normed_s[...] = normed
    pre_inverse_s[...] = jnp.broadcast_to(inverse, normed.shape)
    scaled = normed * gain1[...]
    pre_t[...] = scaled.T.astype(BF16)
    lowered = scaled.astype(BF16)
    gate = dot(lowered, gate_w[...], NN)
    up = dot(lowered, up_w[...], NN)
    silu, sigmoid = silu_parts(gate)
    hidden = (silu * up).astype(BF16)
    hidden_s[...] = hidden
    up_slope[...] = silu.astype(BF16)
    gate_slope[...] = (up * (sigmoid + silu * (1.0 - sigmoid))).astype(BF16)
    updated = cells + dot(hidden, down_w[...], NN)
    normed, inverse = layer_norm(updated)
    post_normed_s[...] = normed
    post_inverse_s[...] = jnp.broadcast_to(inverse, normed.shape)
    post_low[...] = (normed * gain2[...]).astype(BF16)


def weight_kernel(
    received, down_w, gain2, head_t, after, h0, h1, h2, h3, h4, h5, h6,
    weights, updated_out, rows, weights_v, updated_v,
    post_normed, post_inverse, gate_slope, up_slope, pre_t, hidden, post_low, sems, out_sems,
):
    held = (post_normed, post_inverse, gate_slope, up_slope, pre_t, hidden, post_low)
    copies = fetch((h0, h1, h2, h3, h4, h5, h6), held, sems)
    rows[...] = jnp.sum(received[...].astype(F32), axis=0)
    low = jnp.concatenate(
        [rows[pl.ds(step, HEADS, stride=8), :] for step in range(8)], axis=1
    ).astype(BF16)
    post_scaled = dot(low, head_t[...], TN)
    copies[0].wait()
    copies[1].wait()
    updated_grad = norm_backward(post_scaled * gain2[...], post_normed[...], post_inverse[...])
    updated_v[...] = updated_grad
    outs = fetch((updated_v,), (updated_out,), out_sems)
    updated_low = updated_grad.astype(BF16)
    hidden_grad = dot(updated_low, down_w[...], NT)
    for copy in copies[2:]:
        copy.wait()
    gate_low = (hidden_grad * gate_slope[...]).astype(BF16)
    up_low = (hidden_grad * up_slope[...]).astype(BF16)
    gate_part = dot(pre_t[...], gate_low, NN).astype(BF16)
    up_part = dot(pre_t[...], up_low, NN).astype(BF16)
    down_part = dot(updated_low, hidden[...], TN).astype(BF16)
    for block in range(4):
        lanes = slice(block * 128, (block + 1) * 128)
        for first, part in ((0, gate_part), (512, up_part), (1024, down_part)):
            weights_v[first + block * 128 : first + (block + 1) * 128, :] = part[:, lanes]
    weights_v[1536:1552, :] = dot(low, post_low[...], NN).astype(BF16)
    weights_v[1552:, :] = jnp.zeros((CHUNKS * CHUNK_ROWS - 1552, PAIR), BF16)
    last = fetch((weights_v,), (weights,), out_sems.at[pl.ds(1, 1)])
    for copy in (*outs, *last):
        copy.wait()


def inputs_kernel(
    after, updated_grad, gate_slope, up_slope, pre_normed, pre_inverse, gain1, gate_w, up_w, down_w,
    pair_out,
):
    hidden_grad = dot(updated_grad[...].astype(BF16), down_w[...], NT)
    gate_low = (hidden_grad * gate_slope[...]).astype(BF16)
    up_low = (hidden_grad * up_slope[...]).astype(BF16)
    pre_scaled = dot(gate_low, gate_w[...], NT) + dot(up_low, up_w[...], NT)
    inputs_grad = norm_backward(pre_scaled * gain1[...], pre_normed[...], pre_inverse[...])
    result = (updated_grad[...] + inputs_grad).astype(BF16)
    for step in range(8):
        for half in range(2):
            start = step * 128 + half * KEYS
            slab = result[start : start + KEYS]
            pair_out[half * 8 + step] = slab.reshape(2, 32, PAIR)


def sum_kernel(parts, *rest):
    out = rest[-1]
    total = jnp.sum(parts[...].astype(F32), axis=0).astype(out.dtype)
    for j in range(out.shape[0]):
        out[j] = total


def unpack_kernel(
    table, gain1, gate_w, up_w, gain2, head_t,
    gate_out, up_out, down_out, head_out, first_out, second_out,
):
    factor = 1.0 / 512

    def block(k):
        return table[k * 128 : (k + 1) * 128, :].astype(F32) * factor

    total = jnp.zeros((PAIR, 128), F32)
    for k in range(4):
        lanes = slice(k * 128, (k + 1) * 128)
        gate, up = block(k), block(4 + k)
        gate_out[:, lanes] = gate
        up_out[:, lanes] = up
        down_out[lanes, :] = block(8 + k).T
        total = total + gate * gate_w[:, lanes].astype(F32) + up * up_w[:, lanes].astype(F32)
    head = block(12)[:HEADS]
    head_out[...] = head
    first_out[...] = jnp.sum(total.T, axis=0, keepdims=True) / gain1[...]
    second = jnp.sum(head * head_t[...].astype(F32), axis=0, keepdims=True)
    second_out[...] = second / gain2[...]


def shifted(value, axis, shift):
    size = lax.axis_size(axis)
    return lax.ppermute(value, axis, [(i, (i + shift) % size) for i in range(size)])


def all_to_all(value, axes):
    return lax.all_to_all(value, axes, 0, 0, tiled=True)


def local(
    pair_rep, query_rows, key_rows, value_rows, output_grad,
    gain_first, gate_weight, up_weight, down_weight, gain_second, head_weight,
):
    x, zl = lax.axis_index("x"), lax.axis_index("zl")
    y, zh, qi = lax.axis_index("y"), lax.axis_index("zh"), lax.axis_index("qi")
    place = jnp.stack([zl * 4 + x, x, y, zh, qi]).astype(jnp.int32)
    params = (
        gain_first[None], gate_weight, up_weight, down_weight, gain_second[None], head_weight.T,
    )

    def call(kernel, ins, outs, name, scratch=()):
        return pl.pallas_call(
            kernel,
            in_specs=[spec for spec, _ in ins],
            out_specs=[spec for spec, _ in outs],
            out_shape=[out for _, out in outs],
            scratch_shapes=list(scratch),
            compiler_params=PARAMS,
            name=name,
        )(*[value for _, value in ins])

    def vmem(*values):
        return [(VMEM, value) for value in values]

    def kept(*values):
        return [(BLOCK, pltpu.with_memory_space_constraint(v, pltpu.HBM)) for v in values]

    def f32(*dims):
        return (VMEM, jax.ShapeDtypeStruct(dims, F32))

    def bf16(*dims):
        return (VMEM, jax.ShapeDtypeStruct(dims, BF16))

    def f32_kept(*dims):
        return (BLOCK, pltpu.HBM(dims, F32))

    def bf16_kept(*dims):
        return (BLOCK, pltpu.HBM(dims, BF16))

    def in_hbm(value):
        return (HBM, pltpu.with_memory_space_constraint(value, pltpu.HBM))

    (own,) = call(
        bias_kernel,
        [(SMEM, place), in_hbm(pair_rep), *[in_hbm(p) for p in params]],
        [bf16(4, 128, 128)],
        "pair_bias",
        [
            pltpu.VMEM((4, SUB, 2, 32, PAIR), BF16),
            *[pltpu.VMEM(p.shape, p.dtype) for p in params],
            pltpu.VMEM((4, 128, 128), F32),
            pltpu.SemaphoreType.DMA((10,)),
        ],
    )
    first, third, second = [shifted(own, "x", s) for s in (1, 3, 2)]

    scores, attend, query_p, grad_p, wide_keys = call(
        product_kernel,
        vmem(query_rows[0], output_grad[0], key_rows[0], value_rows[0]),
        [
            f32(HEADS * KEYS, ROWS), f32(HEADS * KEYS, ROWS), bf16_kept(ROWS, WIDTH),
            bf16_kept(ROWS, WIDTH), bf16_kept(HEADS * KEYS, WIDTH),
        ],
        "products",
    )

    total, stats = call(
        stats_kernel,
        [(SMEM, place), *vmem(scores, attend, own, first, second, third)],
        [f32(HEADS * KEYS, ROWS), f32(2 * HEADS, ROWS)],
        "softmax_stats",
        [pltpu.VMEM((4, 4, 128, 128), F32)],
    )

    cells = SUB * KEYS
    states = call(
        state_kernel,
        [(SMEM, place), *vmem(total), in_hbm(pair_rep), *vmem(*params)],
        [
            f32_kept(cells, PAIR), f32_kept(cells, PAIR), bf16_kept(cells, FF),
            bf16_kept(cells, FF), bf16_kept(PAIR, cells), bf16_kept(cells, FF),
            bf16_kept(cells, PAIR), f32_kept(cells, PAIR), f32_kept(cells, PAIR),
        ],
        "pair_states",
        [pltpu.VMEM((SUB, 2, 32, PAIR), BF16), pltpu.SemaphoreType.DMA((1,))],
    )

    (merged,) = call(
        merge_kernel,
        [*vmem(stats, shifted(stats, "zh", 1)), in_hbm(states[0])],
        [f32(2 * HEADS, ROWS)],
        "merge_stats",
    )
    peers = [shifted(merged, "y", s) for s in (1, 3, 2)]

    send, score_low, attend_low = call(
        grad_kernel,
        vmem(merged, *peers, total, attend),
        [bf16_kept(16, 128, 128), *[bf16_kept(HEADS * KEYS, ROWS)] * 2],
        "score_grads",
    )

    received = all_to_all(send, NOISE)

    *query_parts, kv_keep, kv_send = call(
        rows_kernel,
        [(SMEM, place), *kept(score_low, attend_low, query_p, grad_p, wide_keys)],
        [*[bf16(2, 32, WIDTH)] * 4, *[f32(32, 2 * WIDTH)] * 2],
        "row_grads",
        [pltpu.VMEM((4, 2, 32, WIDTH), BF16)],
    )

    half = query_parts[0].astype(F32)
    for s in (1, 3, 2):
        half = half + shifted(query_parts[s], "y", s).astype(F32)
    query_sum = half[0] + shifted(half[1].astype(BF16), "zh", 1).astype(F32)
    query_grad = query_sum.astype(BF16)[None]
    kv_sum = (kv_keep + shifted(kv_send, "qi", 1)).astype(BF16)
    key_grad = kv_sum[None, :, :WIDTH]
    value_grad = kv_sum[None, :, WIDTH:]

    weight_rows = CHUNK_ROWS * CHUNKS
    weights, updated_grad = call(
        weight_kernel,
        [
            *vmem(received, *params[3:], half),
            *[in_hbm(v) for v in states[:7]],
        ],
        [
            (HBM, pltpu.HBM((weight_rows, PAIR), BF16)),
            (HBM, pltpu.HBM((cells, PAIR), F32)),
        ],
        "pair_weights",
        [
            pltpu.VMEM((128, 128), F32),
            pltpu.VMEM((weight_rows, PAIR), BF16),
            pltpu.VMEM((cells, PAIR), F32),
            *[pltpu.VMEM(v.shape, v.dtype) for v in states[:7]],
            pltpu.SemaphoreType.DMA((7,)),
            pltpu.SemaphoreType.DMA((2,)),
        ],
    )
    (pair_low,) = call(
        inputs_kernel,
        [in_hbm(weights), *kept(updated_grad, *states[2:4], *states[7:9], *params[:4])],
        [bf16_kept(SUB, 2, 32, PAIR)],
        "pair_inputs",
    )
    pair_grad = pair_low[None, None]
    parts = all_to_all(weights.reshape(CHUNKS, CHUNK_ROWS, PAIR), PLANE)
    (shares,) = call(
        sum_kernel,
        [*vmem(parts), in_hbm(pair_low)],
        [bf16_kept(8, CHUNK_ROWS, PAIR)],
        "plane_sum",
    )
    columns = all_to_all(shares, COLUMN)
    (totals,) = call(
        sum_kernel, vmem(columns), [bf16_kept(CHUNKS, CHUNK_ROWS, PAIR)], "column_sum"
    )
    table = all_to_all(totals, PLANE).reshape(weight_rows, PAIR)
    gate_grad, up_grad, down_grad, head_grad, first_grad, second_grad = call(
        unpack_kernel,
        vmem(table, *params[:3], *params[4:]),
        [
            f32_kept(PAIR, FF), f32_kept(PAIR, FF), f32_kept(FF, PAIR),
            f32_kept(HEADS, PAIR), f32_kept(1, PAIR), f32_kept(1, PAIR),
        ],
        "unpack",
    )
    return (
        query_grad, key_grad, value_grad, pair_grad, gate_grad, up_grad, down_grad,
        head_grad.T, first_grad[0], second_grad[0],
    )


def solution(mesh):
    fine = Mesh(mesh.devices.reshape(4, 4, 2, 2, 4), ("zl", "x", "qi", "zh", "y"))
    kj = ("zh", "y")
    return jax.shard_map(
        local,
        mesh=fine,
        in_specs=(
            P("qi", None, kj, None),
            P(NOISE, "qi", None),
            P(NOISE, None, kj, None),
            P(NOISE, None, kj, None),
            P(NOISE, "qi", None),
            P(),
            P(),
            P(),
            P(),
            P(),
            P(),
        ),
        out_specs=(
            P(NOISE, ("qi", "zh", "y"), None),
            P(NOISE, ("qi", "zh", "y"), None),
            P(NOISE, ("qi", "zh", "y"), None),
            P("qi", NOISE, None, None, kj, None),
            P(),
            P(),
            P(),
            P(),
            P(),
            P(),
        ),
        check_vma=False,
    )
```

```python
import functools

import jax
import jax.numpy as jnp
from jax import lax
from jax.experimental import pallas as pl
from jax.experimental.pallas import tpu as pltpu
from jax.sharding import Mesh, PartitionSpec as P

HEADS = 16
HEAD_DIM = 48
WIDTH = HEADS * HEAD_DIM
PAIR = 128
FF = 512
KEYS = 64
ROWS = 256
SUB = 16
EPSILON = 1e-05
SCALE = HEAD_DIM**-0.5
CHUNK_ROWS = 56
CHUNKS = 32
GROUP = 4
F32 = jnp.float32
BF16 = jnp.bfloat16
NOISE = ("zl", "x")
PLANE = ("x", "qi", "y")
COLUMN = ("zh", "zl")

VMEM = pl.BlockSpec(memory_space=pltpu.VMEM)
SMEM = pl.BlockSpec(memory_space=pltpu.SMEM)
HBM = pl.BlockSpec(memory_space=pltpu.HBM)
BLOCK = pl.BlockSpec()
PARAMS = pltpu.CompilerParams(vmem_limit_bytes=48 * 1024 * 1024)


def dot(left, right, dims):
    return lax.dot_general(left, right, (dims, ((), ())), preferred_element_type=F32)


NN = ((1,), (0,))
NT = ((1,), (1,))
TN = ((0,), (0,))


def layer_norm(values):
    center = values - jnp.mean(values, axis=1, keepdims=True)
    inverse = lax.rsqrt(jnp.mean(center * center, axis=1, keepdims=True) + EPSILON)
    return center * inverse, inverse


def norm_backward(grad, normed, inverse):
    first = jnp.mean(grad, axis=1, keepdims=True)
    second = jnp.mean(grad * normed, axis=1, keepdims=True)
    return inverse * (grad - first - normed * second)


def block_cells(read_row):
    slabs = [read_row(half * 8 + step) for step in range(8) for half in range(2)]
    return jnp.concatenate(slabs, axis=0)


def silu_parts(half):
    curve = jnp.tanh(half)
    return half + half * curve, 0.5 + 0.5 * curve


def fetch(sources, targets, sems):
    copies = [
        pltpu.make_async_copy(source, target, sems.at[k])
        for k, (source, target) in enumerate(zip(sources, targets))
    ]
    for copy in copies:
        copy.start()
    return copies


def bias_kernel(
    place, pair, gain1_h, gate_h, up_h, down_h, gain2_h, head_h, out,
    cells_v, gain1, gate_w, up_w, down_w, gain2, head_t, rows, sems,
):
    x = place[1]
    blocks = [pair.at[pl.ds((zl * 4 + x) * SUB, SUB)] for zl in range(4)]
    copies = fetch(
        (*blocks, gain1_h, gate_h, up_h, down_h, gain2_h, head_h),
        (
            cells_v.at[0], cells_v.at[1], cells_v.at[2], cells_v.at[3],
            gain1, gate_w, up_w, down_w, gain2, head_t,
        ),
        sems,
    )
    for copy in copies[:4]:
        copy.wait()
    for start in range(0, 4, GROUP):
        blocks = range(start, start + GROUP)
        cells = jnp.concatenate(
            [block_cells(lambda r: cells_v[k, r].reshape(KEYS, PAIR)) for k in blocks], axis=0
        ).astype(F32)
        normed, _ = layer_norm(cells)
        if start == 0:
            for copy in copies[4:]:
                copy.wait()
        lowered = (normed * gain1[...]).astype(BF16)
        half = dot(lowered, gate_w[...] * 0.5, NN)
        up = dot(lowered, up_w[...], NN)
        hidden = (silu_parts(half)[0] * up).astype(BF16)
        updated = cells + dot(hidden, down_w[...], NN)
        post, _ = layer_norm(updated)
        post_low = (post * gain2[...]).astype(BF16)
        bias = dot(head_t[...], post_low, NT)
        for place_k, k in enumerate(blocks):
            for step in range(8):
                lane = place_k * 1024 + step * 128
                rows[k, pl.ds(step, HEADS, stride=8), :] = bias[:, lane : lane + 128]
            out[k] = rows[k].astype(BF16)


def head_mask(shape, head):
    column = lax.broadcasted_iota(jnp.int32, shape, 1)
    return (column >= head * HEAD_DIM) & (column < (head + 1) * HEAD_DIM)


def spread_heads(tile):
    wide = tile.astype(F32)
    parts = [
        jnp.where(head_mask(wide.shape, h), wide, 0.0).astype(BF16) for h in range(HEADS)
    ]
    return jnp.concatenate(parts, axis=0)


def permute_rows(tile):
    width = tile.shape[1]
    wide = tile.astype(F32).reshape(16, 2, 8, width)
    parts = [wide[:, half].reshape(128, width) for half in range(2)]
    return jnp.concatenate(parts, axis=0).astype(BF16)


def product_kernel(query, grad, keys, values, scores, attend, query_out, grad_out, keys_out):
    query_p = permute_rows(query[...])
    grad_p = permute_rows(grad[...])
    query_out[...] = query_p
    grad_out[...] = grad_p
    wide_keys = spread_heads(keys[...].reshape(KEYS, WIDTH))
    keys_out[...] = wide_keys
    scores[...] = dot(wide_keys, query_p, NT) * SCALE
    wide_values = spread_heads(values[...].reshape(KEYS, WIDTH))
    attend[...] = dot(wide_values, grad_p, NT)


def stats_kernel(place, scores, attend, own, first, second, third, total_out, stats, wide):
    x = place[1]
    for shift, piece in enumerate((own, first, second, third)):
        origin = lax.rem(x + 4 - shift, 4)
        for zl in range(4):
            wide[zl, origin] = piece[zl].astype(F32)
    logs, means = [], []
    for h in range(HEADS):
        block = wide[:, :, 8 * h : 8 * h + 8, :].reshape(128, 128).T
        bias = jnp.concatenate([block[:KEYS], block[KEYS:]], axis=1)
        rows = slice(h * KEYS, (h + 1) * KEYS)
        total = scores[rows, :] + bias
        total_out[rows, :] = total
        largest = jnp.max(total, axis=0, keepdims=True)
        powers = jnp.exp(total - largest)
        amount = jnp.sum(powers, axis=0, keepdims=True)
        weighted = jnp.sum(powers * attend[rows, :], axis=0, keepdims=True)
        logs.append(largest + jnp.log(amount))
        means.append(weighted / amount)
    stats[...] = jnp.concatenate(logs + means, axis=0)


def merge_stats(parts):
    largest = functools.reduce(jnp.maximum, [p[:HEADS] for p in parts])
    powers = [jnp.exp(p[:HEADS] - largest) for p in parts]
    amount = functools.reduce(jnp.add, powers)
    weighted = functools.reduce(jnp.add, [p[HEADS:] * w for p, w in zip(parts, powers)])
    return largest + jnp.log(amount), weighted / amount


def merge_kernel(own, received, after, merged):
    level, delta = merge_stats([own[...], received[...]])
    merged[:HEADS, :] = level
    merged[HEADS:, :] = delta


def grad_kernel(own, first, second, third, total, attend, send, score_low, attend_low):
    level, delta = merge_stats([own[...], first[...], second[...], third[...]])
    for pair in range(HEADS // 2):
        blocks = []
        for h in (2 * pair, 2 * pair + 1):
            rows = slice(h * KEYS, (h + 1) * KEYS)
            weights = jnp.exp(total[rows, :] - level[h : h + 1])
            score = weights * (attend[rows, :] - delta[h : h + 1])
            score_low[rows, :] = score.astype(BF16)
            attend_low[rows, :] = weights.astype(BF16)
            block = jnp.concatenate([score[:, :128], score[:, 128:]], axis=0).T
            blocks.append(block.reshape(16, 8, 128))
        send[:, 16 * pair : 16 * pair + 16, :] = jnp.concatenate(blocks, axis=1).astype(BF16)


def rows_kernel(
    place, score_low, attend_low, query, grad, keys,
    query_0, query_1, query_2, query_3, kv_keep, kv_send, sends,
):
    y, zh, qi = place[2], place[3], place[4]
    product = dot(score_low[...], keys[...], TN) * SCALE
    for target in range(8):
        rel_z = lax.rem(target // 4 + zh, 2)
        rel_y = lax.rem(target % 4 + 4 - y, 4)
        parts = []
        for block in (2 * target, 2 * target + 1):
            for half in range(2):
                start = half * 128 + block * 8
                parts.append(product[start : start + 8])
        sends[rel_y, rel_z] = jnp.concatenate(parts, axis=0).astype(BF16)
    for shift, out in enumerate((query_0, query_1, query_2, query_3)):
        out[...] = sends[shift]
    for which, (low, rows) in enumerate(((score_low, query), (attend_low, grad))):
        result = jnp.zeros((KEYS, WIDTH), F32)
        for quad in range(4):
            part = dot(low[quad * 256 : quad * 256 + 256, :], rows[...], NN)
            for step in range(4):
                piece = part[step * KEYS : (step + 1) * KEYS]
                mask = head_mask(piece.shape, quad * 4 + step)
                result = result + jnp.where(mask, piece, 0.0)
        if which == 0:
            result = result * SCALE
        lanes = slice(which * WIDTH, (which + 1) * WIDTH)
        first, second = result[:32], result[32:]
        kv_keep[:, lanes] = jnp.where(qi == 0, first, second)
        kv_send[:, lanes] = jnp.where(qi == 0, second, first)


def state_kernel(
    place, after, pair, gain1, gate_w, up_w, down_w, gain2, head_t,
    post_normed_s, post_inverse_s, gate_slope, up_slope, pre_t, hidden_s, post_low,
    cells_v, sems,
):
    for copy in fetch((pair.at[pl.ds(place[0] * SUB, SUB)],), (cells_v,), sems):
        copy.wait()
    cells = block_cells(lambda r: cells_v[r].reshape(KEYS, PAIR)).astype(F32)
    normed, _ = layer_norm(cells)
    scaled = normed * gain1[...]
    pre_t[...] = scaled.T.astype(BF16)
    lowered = scaled.astype(BF16)
    half = dot(lowered, gate_w[...] * 0.5, NN)
    up = dot(lowered, up_w[...], NN)
    silu, sigmoid = silu_parts(half)
    hidden = (silu * up).astype(BF16)
    hidden_s[...] = hidden
    up_slope[...] = silu.astype(BF16)
    gate_slope[...] = (up * (sigmoid + silu * (1.0 - sigmoid))).astype(BF16)
    updated = cells + dot(hidden, down_w[...], NN)
    normed, inverse = layer_norm(updated)
    post_normed_s[...] = normed
    post_inverse_s[...] = jnp.broadcast_to(inverse, normed.shape)
    post_low[...] = (normed * gain2[...]).astype(BF16)


def weight_kernel(
    received, down_w, gain2, head_t, after, h0, h1, h2, h3, h4, h5, h6,
    weights, updated_out, rows, weights_v, updated_v,
    post_normed, post_inverse, gate_slope, up_slope, pre_t, hidden, post_low, sems, out_sems,
):
    held = (post_normed, post_inverse, gate_slope, up_slope, pre_t, hidden, post_low)
    copies = fetch((h0, h1, h2, h3, h4, h5, h6), held, sems)
    rows[...] = jnp.sum(received[...].astype(F32), axis=0)
    low = jnp.concatenate(
        [rows[pl.ds(step, HEADS, stride=8), :] for step in range(8)], axis=1
    ).astype(BF16)
    post_scaled = dot(low, head_t[...], TN)
    copies[0].wait()
    copies[1].wait()
    updated_grad = norm_backward(post_scaled * gain2[...], post_normed[...], post_inverse[...])
    updated_v[...] = updated_grad
    outs = fetch((updated_v,), (updated_out,), out_sems)
    updated_low = updated_grad.astype(BF16)
    hidden_grad = dot(updated_low, down_w[...], NT)
    for copy in copies[2:]:
        copy.wait()
    gate_low = (hidden_grad * gate_slope[...]).astype(BF16)
    up_low = (hidden_grad * up_slope[...]).astype(BF16)
    def give(first, rows_of, k):
        part = pl.ds(first, rows_of)
        outs.extend(fetch((weights_v.at[part],), (weights.at[part],), out_sems.at[pl.ds(k, 1)]))

    def place_part(first, part, k):
        for block in range(4):
            lanes = slice(block * 128, (block + 1) * 128)
            weights_v[first + block * 128 : first + (block + 1) * 128, :] = part[:, lanes]
        give(first, 512, k)

    rest = CHUNKS * CHUNK_ROWS - 1536
    weights_v[1536:1552, :] = dot(low, post_low[...], NN).astype(BF16)
    weights_v[1552:, :] = jnp.zeros((rest - 16, PAIR), BF16)
    give(1536, rest, 1)
    place_part(1024, dot(updated_low, hidden[...], TN).astype(BF16), 2)
    place_part(0, dot(pre_t[...], gate_low, NN).astype(BF16), 3)
    place_part(512, dot(pre_t[...], up_low, NN).astype(BF16), 4)
    for copy in outs:
        copy.wait()


def inputs_kernel(
    place, after, pair, updated_grad, gate_slope, up_slope, gain1, gate_w, up_w, down_w,
    pair_out, cells_v, sems,
):
    copies = fetch((pair.at[pl.ds(place[0] * SUB, SUB)],), (cells_v,), sems)
    hidden_grad = dot(updated_grad[...].astype(BF16), down_w[...], NT)
    gate_low = (hidden_grad * gate_slope[...]).astype(BF16)
    up_low = (hidden_grad * up_slope[...]).astype(BF16)
    pre_scaled = dot(gate_low, gate_w[...], NT) + dot(up_low, up_w[...], NT)
    for copy in copies:
        copy.wait()
    cells = block_cells(lambda r: cells_v[r].reshape(KEYS, PAIR)).astype(F32)
    inputs_grad = norm_backward(pre_scaled * gain1[...], *layer_norm(cells))
    result = (updated_grad[...] + inputs_grad).astype(BF16)
    for step in range(8):
        for half in range(2):
            start = step * 128 + half * KEYS
            slab = result[start : start + KEYS]
            pair_out[half * 8 + step] = slab.reshape(2, 32, PAIR)


def sum_kernel(parts, out):
    total = jnp.sum(parts[...].astype(F32), axis=0).astype(out.dtype)
    for j in range(out.shape[0]):
        out[j] = total


def unpack_kernel(
    table, gain1, gate_w, up_w, gain2, head_t,
    gate_out, up_out, down_out, head_out, first_out, second_out,
):
    factor = 1.0 / 512

    def block(k):
        return table[k * 128 : (k + 1) * 128, :].astype(F32) * factor

    total = jnp.zeros((PAIR, 128), F32)
    for k in range(4):
        lanes = slice(k * 128, (k + 1) * 128)
        gate, up = block(k), block(4 + k)
        gate_out[:, lanes] = gate
        up_out[:, lanes] = up
        down_out[lanes, :] = block(8 + k).T
        total = total + gate * gate_w[:, lanes].astype(F32) + up * up_w[:, lanes].astype(F32)
    head = block(12)[:HEADS]
    head_out[...] = head
    first_out[...] = jnp.sum(total.T, axis=0, keepdims=True) / gain1[...]
    second = jnp.sum(head * head_t[...].astype(F32), axis=0, keepdims=True)
    second_out[...] = second / gain2[...]


def shifted(value, axis, shift):
    size = lax.axis_size(axis)
    return lax.ppermute(value, axis, [(i, (i + shift) % size) for i in range(size)])


def all_to_all(value, axes):
    return lax.all_to_all(value, axes, 0, 0, tiled=True)


def local(
    pair_rep, query_rows, key_rows, value_rows, output_grad,
    gain_first, gate_weight, up_weight, down_weight, gain_second, head_weight,
):
    x, zl = lax.axis_index("x"), lax.axis_index("zl")
    y, zh, qi = lax.axis_index("y"), lax.axis_index("zh"), lax.axis_index("qi")
    place = jnp.stack([zl * 4 + x, x, y, zh, qi]).astype(jnp.int32)
    params = (
        gain_first[None], gate_weight, up_weight, down_weight, gain_second[None], head_weight.T,
    )

    def call(kernel, ins, outs, name, scratch=()):
        return pl.pallas_call(
            kernel,
            in_specs=[spec for spec, _ in ins],
            out_specs=[spec for spec, _ in outs],
            out_shape=[out for _, out in outs],
            scratch_shapes=list(scratch),
            compiler_params=PARAMS,
            name=name,
        )(*[value for _, value in ins])

    def vmem(*values):
        return [(VMEM, value) for value in values]

    def kept(*values):
        return [(BLOCK, pltpu.with_memory_space_constraint(v, pltpu.HBM)) for v in values]

    def f32(*dims):
        return (VMEM, jax.ShapeDtypeStruct(dims, F32))

    def bf16(*dims):
        return (VMEM, jax.ShapeDtypeStruct(dims, BF16))

    def f32_kept(*dims):
        return (BLOCK, pltpu.HBM(dims, F32))

    def bf16_kept(*dims):
        return (BLOCK, pltpu.HBM(dims, BF16))

    def in_hbm(value):
        return (HBM, pltpu.with_memory_space_constraint(value, pltpu.HBM))

    (own,) = call(
        bias_kernel,
        [(SMEM, place), in_hbm(pair_rep), *[in_hbm(p) for p in params]],
        [bf16(4, 128, 128)],
        "pair_bias",
        [
            pltpu.VMEM((4, SUB, 2, 32, PAIR), BF16),
            *[pltpu.VMEM(p.shape, p.dtype) for p in params],
            pltpu.VMEM((4, 128, 128), F32),
            pltpu.SemaphoreType.DMA((10,)),
        ],
    )
    first, third, second = [shifted(own, "x", s) for s in (1, 3, 2)]

    scores, attend, query_p, grad_p, wide_keys = call(
        product_kernel,
        vmem(query_rows[0], output_grad[0], key_rows[0], value_rows[0]),
        [
            f32(HEADS * KEYS, ROWS), f32(HEADS * KEYS, ROWS), bf16_kept(ROWS, WIDTH),
            bf16_kept(ROWS, WIDTH), bf16_kept(HEADS * KEYS, WIDTH),
        ],
        "products",
    )

    total, stats = call(
        stats_kernel,
        [(SMEM, place), *vmem(scores, attend, own, first, second, third)],
        [f32(HEADS * KEYS, ROWS), f32(2 * HEADS, ROWS)],
        "softmax_stats",
        [pltpu.VMEM((4, 4, 128, 128), F32)],
    )

    cells = SUB * KEYS
    states = call(
        state_kernel,
        [(SMEM, place), *vmem(total), in_hbm(pair_rep), *vmem(*params)],
        [
            f32_kept(cells, PAIR), f32_kept(cells, PAIR), bf16_kept(cells, FF),
            bf16_kept(cells, FF), bf16_kept(PAIR, cells), bf16_kept(cells, FF),
            bf16_kept(cells, PAIR),
        ],
        "pair_states",
        [pltpu.VMEM((SUB, 2, 32, PAIR), BF16), pltpu.SemaphoreType.DMA((1,))],
    )

    (merged,) = call(
        merge_kernel,
        [*vmem(stats, shifted(stats, "zh", 1)), in_hbm(states[0])],
        [f32(2 * HEADS, ROWS)],
        "merge_stats",
    )
    peers = [shifted(merged, "y", s) for s in (1, 3, 2)]

    send, score_low, attend_low = call(
        grad_kernel,
        vmem(merged, *peers, total, attend),
        [bf16_kept(16, 128, 128), *[bf16_kept(HEADS * KEYS, ROWS)] * 2],
        "score_grads",
    )

    received = all_to_all(send, NOISE)

    *query_parts, kv_keep, kv_send = call(
        rows_kernel,
        [(SMEM, place), *kept(score_low, attend_low, query_p, grad_p, wide_keys)],
        [*[bf16(2, 32, WIDTH)] * 4, *[f32(32, 2 * WIDTH)] * 2],
        "row_grads",
        [pltpu.VMEM((4, 2, 32, WIDTH), BF16)],
    )

    half = query_parts[0].astype(F32)
    for s in (1, 3, 2):
        half = half + shifted(query_parts[s], "y", s).astype(F32)
    query_sum = half[0] + shifted(half[1].astype(BF16), "zh", 1).astype(F32)
    query_grad = query_sum.astype(BF16)[None]
    kv_sum = (kv_keep + shifted(kv_send, "qi", 1)).astype(BF16)
    key_grad = kv_sum[None, :, :WIDTH]
    value_grad = kv_sum[None, :, WIDTH:]

    weight_rows = CHUNK_ROWS * CHUNKS
    weights, updated_grad = call(
        weight_kernel,
        [
            *vmem(received, *params[3:], half),
            *[in_hbm(v) for v in states[:7]],
        ],
        [
            (HBM, pltpu.HBM((weight_rows, PAIR), BF16)),
            (HBM, pltpu.HBM((cells, PAIR), F32)),
        ],
        "pair_weights",
        [
            pltpu.VMEM((128, 128), F32),
            pltpu.VMEM((weight_rows, PAIR), BF16),
            pltpu.VMEM((cells, PAIR), F32),
            *[pltpu.VMEM(v.shape, v.dtype) for v in states[:7]],
            pltpu.SemaphoreType.DMA((7,)),
            pltpu.SemaphoreType.DMA((5,)),
        ],
    )
    parts = all_to_all(weights.reshape(CHUNKS, CHUNK_ROWS, PAIR), PLANE)
    (shares,) = call(
        sum_kernel,
        vmem(parts),
        [bf16_kept(8, CHUNK_ROWS, PAIR)],
        "plane_sum",
    )
    columns = all_to_all(shares, COLUMN)
    (totals,) = call(
        sum_kernel, vmem(columns), [bf16_kept(CHUNKS, CHUNK_ROWS, PAIR)], "column_sum"
    )
    (pair_low,) = call(
        inputs_kernel,
        [
            (SMEM, place), in_hbm(totals), in_hbm(pair_rep),
            *kept(updated_grad, *states[2:4], *params[:4]),
        ],
        [bf16_kept(SUB, 2, 32, PAIR)],
        "pair_inputs",
        [pltpu.VMEM((SUB, 2, 32, PAIR), BF16), pltpu.SemaphoreType.DMA((1,))],
    )
    pair_grad = pair_low[None, None]
    table = all_to_all(totals, PLANE).reshape(weight_rows, PAIR)
    gate_grad, up_grad, down_grad, head_grad, first_grad, second_grad = call(
        unpack_kernel,
        vmem(table, *params[:3], *params[4:]),
        [
            f32_kept(PAIR, FF), f32_kept(PAIR, FF), f32_kept(FF, PAIR),
            f32_kept(HEADS, PAIR), f32_kept(1, PAIR), f32_kept(1, PAIR),
        ],
        "unpack",
    )
    return (
        query_grad, key_grad, value_grad, pair_grad, gate_grad, up_grad, down_grad,
        head_grad.T, first_grad[0], second_grad[0],
    )


def solution(mesh):
    fine = Mesh(mesh.devices.reshape(4, 4, 2, 2, 4), ("zl", "x", "qi", "zh", "y"))
    kj = ("zh", "y")
    return jax.shard_map(
        local,
        mesh=fine,
        in_specs=(
            P("qi", None, kj, None),
            P(NOISE, "qi", None),
            P(NOISE, None, kj, None),
            P(NOISE, None, kj, None),
            P(NOISE, "qi", None),
            P(),
            P(),
            P(),
            P(),
            P(),
            P(),
        ),
        out_specs=(
            P(NOISE, ("qi", "zh", "y"), None),
            P(NOISE, ("qi", "zh", "y"), None),
            P(NOISE, ("qi", "zh", "y"), None),
            P("qi", NOISE, None, None, kj, None),
            P(),
            P(),
            P(),
            P(),
            P(),
            P(),
        ),
        check_vma=False,
    )
```

```python
import functools

import jax
import jax.numpy as jnp
from jax import lax
from jax.experimental import pallas as pl
from jax.experimental.pallas import tpu as pltpu
from jax.sharding import Mesh, PartitionSpec as P

HEADS = 16
HEAD_DIM = 48
WIDTH = HEADS * HEAD_DIM
PAIR = 128
FF = 512
KEYS = 64
ROWS = 256
SUB = 16
EPSILON = 1e-05
SCALE = HEAD_DIM**-0.5
CHUNK_ROWS = 56
CHUNKS = 32
GROUP = 2
F32 = jnp.float32
BF16 = jnp.bfloat16
NOISE = ("zl", "x")
PLANE = ("x", "qi", "y")
COLUMN = ("zh", "zl")

VMEM = pl.BlockSpec(memory_space=pltpu.VMEM)
SMEM = pl.BlockSpec(memory_space=pltpu.SMEM)
HBM = pl.BlockSpec(memory_space=pltpu.HBM)
BLOCK = pl.BlockSpec()
PARAMS = pltpu.CompilerParams(vmem_limit_bytes=48 * 1024 * 1024)


def dot(left, right, dims):
    return lax.dot_general(left, right, (dims, ((), ())), preferred_element_type=F32)


NN = ((1,), (0,))
NT = ((1,), (1,))
TN = ((0,), (0,))


def layer_norm(values):
    center = values - jnp.mean(values, axis=1, keepdims=True)
    inverse = lax.rsqrt(jnp.mean(center * center, axis=1, keepdims=True) + EPSILON)
    return center * inverse, inverse


def centering_matrix():
    row = lax.broadcasted_iota(jnp.int32, (PAIR, PAIR), 0)
    column = lax.broadcasted_iota(jnp.int32, (PAIR, PAIR), 1)
    return (jnp.where(row == column, 1.0, 0.0) - 1.0 / PAIR).astype(BF16)


def centered_norm(cells, centering):
    center = dot(cells, centering, NN)
    inverse = lax.rsqrt(jnp.mean(center * center, axis=1, keepdims=True) + EPSILON)
    return center * inverse, inverse


def norm_backward(grad, normed, inverse):
    first = jnp.mean(grad, axis=1, keepdims=True)
    second = jnp.mean(grad * normed, axis=1, keepdims=True)
    return inverse * (grad - first - normed * second)


def block_cells(read_row):
    slabs = [read_row(half * 8 + step) for step in range(8) for half in range(2)]
    return jnp.concatenate(slabs, axis=0)


def silu_parts(half):
    curve = jnp.tanh(half)
    return half + half * curve, 0.5 + 0.5 * curve


def fetch(sources, targets, sems):
    copies = [
        pltpu.make_async_copy(source, target, sems.at[k])
        for k, (source, target) in enumerate(zip(sources, targets))
    ]
    for copy in copies:
        copy.start()
    return copies


def bias_kernel(
    place, pair, gain1_h, gate_h, up_h, down_h, gain2_h, head_h, out,
    cells_v, gain1, gate_w, up_w, down_w, gain2, head_t, rows, sems,
):
    x = place[1]
    blocks = [pair.at[pl.ds((zl * 4 + x) * SUB, SUB)] for zl in range(4)]
    copies = fetch(
        (*blocks, gain1_h, gate_h, up_h, down_h, gain2_h, head_h),
        (
            cells_v.at[0], cells_v.at[1], cells_v.at[2], cells_v.at[3],
            gain1, gate_w, up_w, down_w, gain2, head_t,
        ),
        sems,
    )
    for copy in copies:
        copy.wait()
    centering = centering_matrix()
    groups = [range(start, start + GROUP) for start in range(0, 4, GROUP)]

    def normed_cells(blocks):
        cells = jnp.concatenate(
            [block_cells(lambda r: cells_v[k, r].reshape(KEYS, PAIR)) for k in blocks], axis=0
        )
        return cells.astype(F32), centered_norm(cells, centering)[0]

    def project(cells, normed):
        lowered = (normed * gain1[...]).astype(BF16)
        return cells, dot(lowered, gate_w[...] * 0.5, NN), dot(lowered, up_w[...], NN)

    def activate(cells, half, up):
        return cells, (silu_parts(half)[0] * up).astype(BF16)

    def update(cells, hidden):
        return (cells + dot(hidden, down_w[...], NN),)

    def lower(updated):
        return ((layer_norm(updated)[0] * gain2[...]).astype(BF16),)

    stages = (project, activate, update, lower)
    held = [None] * len(groups)
    for step in range(len(groups) + len(stages)):
        for index, blocks in enumerate(groups):
            stage = step - index
            if stage == 0:
                held[index] = normed_cells(blocks)
            elif 0 < stage <= len(stages):
                held[index] = stages[stage - 1](*held[index])
            if stage == len(stages):
                bias = dot(head_t[...], held[index][0], NT)
                for order, k in enumerate(blocks):
                    for row in range(8):
                        lane = order * 1024 + row * 128
                        rows[k, pl.ds(row, HEADS, stride=8), :] = bias[:, lane : lane + 128]
                    out[k] = rows[k].astype(BF16)


def head_mask(shape, head):
    column = lax.broadcasted_iota(jnp.int32, shape, 1)
    return (column >= head * HEAD_DIM) & (column < (head + 1) * HEAD_DIM)


def spread_heads(tile):
    wide = tile.astype(F32)
    parts = [
        jnp.where(head_mask(wide.shape, h), wide, 0.0).astype(BF16) for h in range(HEADS)
    ]
    return jnp.concatenate(parts, axis=0)


def permute_rows(tile):
    width = tile.shape[1]
    wide = tile.astype(F32).reshape(16, 2, 8, width)
    parts = [wide[:, half].reshape(128, width) for half in range(2)]
    return jnp.concatenate(parts, axis=0).astype(BF16)


def product_kernel(query, grad, keys, values, scores, attend, query_out, grad_out, keys_out):
    query_p = permute_rows(query[...])
    grad_p = permute_rows(grad[...])
    query_out[...] = query_p
    grad_out[...] = grad_p
    wide_keys = spread_heads(keys[...].reshape(KEYS, WIDTH))
    keys_out[...] = wide_keys
    scores[...] = dot(wide_keys, query_p, NT) * SCALE
    wide_values = spread_heads(values[...].reshape(KEYS, WIDTH))
    attend[...] = dot(wide_values, grad_p, NT)


def stats_kernel(place, scores, attend, own, first, second, third, total_out, stats, wide):
    x = place[1]
    for shift, piece in enumerate((own, first, second, third)):
        origin = lax.rem(x + 4 - shift, 4)
        for zl in range(4):
            wide[zl, origin] = piece[zl].astype(F32)
    logs, means = [], []
    for h in range(HEADS):
        block = wide[:, :, 8 * h : 8 * h + 8, :].reshape(128, 128).T
        bias = jnp.concatenate([block[:KEYS], block[KEYS:]], axis=1)
        rows = slice(h * KEYS, (h + 1) * KEYS)
        total = scores[rows, :] + bias
        total_out[rows, :] = total
        largest = jnp.max(total, axis=0, keepdims=True)
        powers = jnp.exp(total - largest)
        amount = jnp.sum(powers, axis=0, keepdims=True)
        weighted = jnp.sum(powers * attend[rows, :], axis=0, keepdims=True)
        logs.append(largest + jnp.log(amount))
        means.append(weighted / amount)
    stats[...] = jnp.concatenate(logs + means, axis=0)


def merge_stats(parts):
    largest = functools.reduce(jnp.maximum, [p[:HEADS] for p in parts])
    powers = [jnp.exp(p[:HEADS] - largest) for p in parts]
    amount = functools.reduce(jnp.add, powers)
    weighted = functools.reduce(jnp.add, [p[HEADS:] * w for p, w in zip(parts, powers)])
    return largest + jnp.log(amount), weighted / amount


def merge_kernel(own, received, after, merged):
    level, delta = merge_stats([own[...], received[...]])
    merged[:HEADS, :] = level
    merged[HEADS:, :] = delta


def grad_kernel(own, first, second, third, total, attend, send, score_low, attend_low):
    level, delta = merge_stats([own[...], first[...], second[...], third[...]])
    for pair in range(HEADS // 2):
        blocks = []
        for h in (2 * pair, 2 * pair + 1):
            rows = slice(h * KEYS, (h + 1) * KEYS)
            weights = jnp.exp(total[rows, :] - level[h : h + 1])
            score = weights * (attend[rows, :] - delta[h : h + 1])
            score_low[rows, :] = score.astype(BF16)
            attend_low[rows, :] = weights.astype(BF16)
            block = jnp.concatenate([score[:, :128], score[:, 128:]], axis=0).T
            blocks.append(block.reshape(16, 8, 128))
        send[:, 16 * pair : 16 * pair + 16, :] = jnp.concatenate(blocks, axis=1).astype(BF16)


def rows_kernel(
    place, score_low, attend_low, query, grad, keys,
    query_0, query_1, query_2, query_3, kv_keep, kv_send, sends,
):
    y, zh, qi = place[2], place[3], place[4]
    product = dot(score_low[...], keys[...], TN) * SCALE
    for target in range(8):
        rel_z = lax.rem(target // 4 + zh, 2)
        rel_y = lax.rem(target % 4 + 4 - y, 4)
        parts = []
        for block in (2 * target, 2 * target + 1):
            for half in range(2):
                start = half * 128 + block * 8
                parts.append(product[start : start + 8])
        sends[rel_y, rel_z] = jnp.concatenate(parts, axis=0).astype(BF16)
    for shift, out in enumerate((query_0, query_1, query_2, query_3)):
        out[...] = sends[shift]
    for which, (low, rows) in enumerate(((score_low, query), (attend_low, grad))):
        result = jnp.zeros((KEYS, WIDTH), F32)
        for quad in range(4):
            part = dot(low[quad * 256 : quad * 256 + 256, :], rows[...], NN)
            for step in range(4):
                piece = part[step * KEYS : (step + 1) * KEYS]
                mask = head_mask(piece.shape, quad * 4 + step)
                result = result + jnp.where(mask, piece, 0.0)
        if which == 0:
            result = result * SCALE
        lanes = slice(which * WIDTH, (which + 1) * WIDTH)
        first, second = result[:32], result[32:]
        kv_keep[:, lanes] = jnp.where(qi == 0, first, second)
        kv_send[:, lanes] = jnp.where(qi == 0, second, first)


def state_kernel(
    place, after, pair, gain1, gate_w, up_w, down_w, gain2, head_t,
    post_normed_s, post_inverse_s, gate_slope, up_slope, pre_t, hidden_s, post_low,
    cells_v, sems,
):
    for copy in fetch((pair.at[pl.ds(place[0] * SUB, SUB)],), (cells_v,), sems):
        copy.wait()
    low_cells = block_cells(lambda r: cells_v[r].reshape(KEYS, PAIR))
    cells = low_cells.astype(F32)
    normed, _ = centered_norm(low_cells, centering_matrix())
    scaled = normed * gain1[...]
    pre_t[...] = scaled.T.astype(BF16)
    lowered = scaled.astype(BF16)
    half = dot(lowered, gate_w[...] * 0.5, NN)
    up = dot(lowered, up_w[...], NN)
    silu, sigmoid = silu_parts(half)
    hidden = (silu * up).astype(BF16)
    hidden_s[...] = hidden
    up_slope[...] = silu.astype(BF16)
    gate_slope[...] = (up * (sigmoid + silu * (1.0 - sigmoid))).astype(BF16)
    updated = cells + dot(hidden, down_w[...], NN)
    normed, inverse = layer_norm(updated)
    post_normed_s[...] = normed
    post_inverse_s[...] = jnp.broadcast_to(inverse, normed.shape)
    post_low[...] = (normed * gain2[...]).astype(BF16)


def weight_kernel(
    received, down_w, gain2, head_t, after, h0, h1, h2, h3, h4, h5, h6,
    weights, updated_out, rows, weights_v, updated_v,
    post_normed, post_inverse, gate_slope, up_slope, pre_t, hidden, post_low, sems, out_sems,
):
    held = (post_normed, post_inverse, gate_slope, up_slope, pre_t, hidden, post_low)
    copies = fetch((h0, h1, h2, h3, h4, h5, h6), held, sems)
    rows[...] = jnp.sum(received[...].astype(F32), axis=0)
    low = jnp.concatenate(
        [rows[pl.ds(step, HEADS, stride=8), :] for step in range(8)], axis=1
    ).astype(BF16)
    spans = [slice(start, start + 512) for start in (0, 512)]
    post_scaled = [dot(low[:, span], head_t[...], TN) for span in spans]
    copies[0].wait()
    copies[1].wait()
    updated_grads = [
        norm_backward(scaled * gain2[...], post_normed[span, :], post_inverse[span, :])
        for scaled, span in zip(post_scaled, spans)
    ]
    for grad, span in zip(updated_grads, spans):
        updated_v[span, :] = grad
    outs = fetch((updated_v,), (updated_out,), out_sems)
    updated_lows = [grad.astype(BF16) for grad in updated_grads]
    hidden_grads = [dot(grad, down_w[...], NT) for grad in updated_lows]
    for copy in copies[2:]:
        copy.wait()
    gate_low = jnp.concatenate(
        [(g * gate_slope[span, :]).astype(BF16) for g, span in zip(hidden_grads, spans)], axis=0
    )
    up_low = jnp.concatenate(
        [(g * up_slope[span, :]).astype(BF16) for g, span in zip(hidden_grads, spans)], axis=0
    )
    updated_low = jnp.concatenate(updated_lows, axis=0)

    def give(first, rows_of, k):
        part = pl.ds(first, rows_of)
        outs.extend(fetch((weights_v.at[part],), (weights.at[part],), out_sems.at[pl.ds(k, 1)]))

    def place_part(first, part, k):
        for block in range(4):
            lanes = slice(block * 128, (block + 1) * 128)
            weights_v[first + block * 128 : first + (block + 1) * 128, :] = part[:, lanes]
        give(first, 512, k)

    rest = CHUNKS * CHUNK_ROWS - 1536
    weights_v[1536:1552, :] = dot(low, post_low[...], NN).astype(BF16)
    weights_v[1552:, :] = jnp.zeros((rest - 16, PAIR), BF16)
    give(1536, rest, 1)
    place_part(1024, dot(updated_low, hidden[...], TN).astype(BF16), 2)
    place_part(0, dot(pre_t[...], gate_low, NN).astype(BF16), 3)
    place_part(512, dot(pre_t[...], up_low, NN).astype(BF16), 4)
    for copy in outs:
        copy.wait()


def inputs_kernel(
    place, after, pair, updated_grad, gate_slope, up_slope, gain1, gate_w, up_w, down_w,
    pair_out, cells_v, sems,
):
    copies = fetch((pair.at[pl.ds(place[0] * SUB, SUB)],), (cells_v,), sems)
    hidden_grad = dot(updated_grad[...].astype(BF16), down_w[...], NT)
    gate_low = (hidden_grad * gate_slope[...]).astype(BF16)
    up_low = (hidden_grad * up_slope[...]).astype(BF16)
    pre_scaled = dot(gate_low, gate_w[...], NT) + dot(up_low, up_w[...], NT)
    for copy in copies:
        copy.wait()
    cells = block_cells(lambda r: cells_v[r].reshape(KEYS, PAIR)).astype(F32)
    inputs_grad = norm_backward(pre_scaled * gain1[...], *layer_norm(cells))
    result = (updated_grad[...] + inputs_grad).astype(BF16)
    for step in range(8):
        for half in range(2):
            start = step * 128 + half * KEYS
            slab = result[start : start + KEYS]
            pair_out[half * 8 + step] = slab.reshape(2, 32, PAIR)


def sum_kernel(parts, out):
    total = jnp.sum(parts[...].astype(F32), axis=0).astype(out.dtype)
    for j in range(out.shape[0]):
        out[j] = total


def unpack_kernel(
    table, gain1, gate_w, up_w, gain2, head_t,
    gate_out, up_out, down_out, head_out, first_out, second_out,
):
    factor = 1.0 / 512

    def block(k):
        return table[k * 128 : (k + 1) * 128, :].astype(F32) * factor

    total = jnp.zeros((PAIR, 128), F32)
    for k in range(4):
        lanes = slice(k * 128, (k + 1) * 128)
        gate, up = block(k), block(4 + k)
        gate_out[:, lanes] = gate
        up_out[:, lanes] = up
        down_out[lanes, :] = block(8 + k).T
        total = total + gate * gate_w[:, lanes].astype(F32) + up * up_w[:, lanes].astype(F32)
    head = block(12)[:HEADS]
    head_out[...] = head
    first_out[...] = jnp.sum(total.T, axis=0, keepdims=True) / gain1[...]
    second = jnp.sum(head * head_t[...].astype(F32), axis=0, keepdims=True)
    second_out[...] = second / gain2[...]


def shifted(value, axis, shift):
    size = lax.axis_size(axis)
    return lax.ppermute(value, axis, [(i, (i + shift) % size) for i in range(size)])


def all_to_all(value, axes):
    return lax.all_to_all(value, axes, 0, 0, tiled=True)


def local(
    pair_rep, query_rows, key_rows, value_rows, output_grad,
    gain_first, gate_weight, up_weight, down_weight, gain_second, head_weight,
):
    x, zl = lax.axis_index("x"), lax.axis_index("zl")
    y, zh, qi = lax.axis_index("y"), lax.axis_index("zh"), lax.axis_index("qi")
    place = jnp.stack([zl * 4 + x, x, y, zh, qi]).astype(jnp.int32)
    params = (
        gain_first[None], gate_weight, up_weight, down_weight, gain_second[None], head_weight.T,
    )

    def call(kernel, ins, outs, name, scratch=()):
        return pl.pallas_call(
            kernel,
            in_specs=[spec for spec, _ in ins],
            out_specs=[spec for spec, _ in outs],
            out_shape=[out for _, out in outs],
            scratch_shapes=list(scratch),
            compiler_params=PARAMS,
            name=name,
        )(*[value for _, value in ins])

    def vmem(*values):
        return [(VMEM, value) for value in values]

    def kept(*values):
        return [(BLOCK, pltpu.with_memory_space_constraint(v, pltpu.HBM)) for v in values]

    def f32(*dims):
        return (VMEM, jax.ShapeDtypeStruct(dims, F32))

    def bf16(*dims):
        return (VMEM, jax.ShapeDtypeStruct(dims, BF16))

    def f32_kept(*dims):
        return (BLOCK, pltpu.HBM(dims, F32))

    def bf16_kept(*dims):
        return (BLOCK, pltpu.HBM(dims, BF16))

    def in_hbm(value):
        return (HBM, pltpu.with_memory_space_constraint(value, pltpu.HBM))

    (own,) = call(
        bias_kernel,
        [(SMEM, place), in_hbm(pair_rep), *[in_hbm(p) for p in params]],
        [bf16(4, 128, 128)],
        "pair_bias",
        [
            pltpu.VMEM((4, SUB, 2, 32, PAIR), BF16),
            *[pltpu.VMEM(p.shape, p.dtype) for p in params],
            pltpu.VMEM((4, 128, 128), F32),
            pltpu.SemaphoreType.DMA((10,)),
        ],
    )
    first, third, second = [shifted(own, "x", s) for s in (1, 3, 2)]

    scores, attend, query_p, grad_p, wide_keys = call(
        product_kernel,
        vmem(query_rows[0], output_grad[0], key_rows[0], value_rows[0]),
        [
            f32(HEADS * KEYS, ROWS), f32(HEADS * KEYS, ROWS), bf16_kept(ROWS, WIDTH),
            bf16_kept(ROWS, WIDTH), bf16_kept(HEADS * KEYS, WIDTH),
        ],
        "products",
    )

    total, stats = call(
        stats_kernel,
        [(SMEM, place), *vmem(scores, attend, own, first, second, third)],
        [f32(HEADS * KEYS, ROWS), f32(2 * HEADS, ROWS)],
        "softmax_stats",
        [pltpu.VMEM((4, 4, 128, 128), F32)],
    )

    cells = SUB * KEYS
    states = call(
        state_kernel,
        [(SMEM, place), *vmem(total), in_hbm(pair_rep), *vmem(*params)],
        [
            f32_kept(cells, PAIR), f32_kept(cells, PAIR), bf16_kept(cells, FF),
            bf16_kept(cells, FF), bf16_kept(PAIR, cells), bf16_kept(cells, FF),
            bf16_kept(cells, PAIR),
        ],
        "pair_states",
        [pltpu.VMEM((SUB, 2, 32, PAIR), BF16), pltpu.SemaphoreType.DMA((1,))],
    )

    (merged,) = call(
        merge_kernel,
        [*vmem(stats, shifted(stats, "zh", 1)), in_hbm(states[0])],
        [f32(2 * HEADS, ROWS)],
        "merge_stats",
    )
    peers = [shifted(merged, "y", s) for s in (1, 3, 2)]

    send, score_low, attend_low = call(
        grad_kernel,
        vmem(merged, *peers, total, attend),
        [bf16_kept(16, 128, 128), *[bf16_kept(HEADS * KEYS, ROWS)] * 2],
        "score_grads",
    )

    received = all_to_all(send, NOISE)

    *query_parts, kv_keep, kv_send = call(
        rows_kernel,
        [(SMEM, place), *kept(score_low, attend_low, query_p, grad_p, wide_keys)],
        [*[bf16(2, 32, WIDTH)] * 4, *[f32(32, 2 * WIDTH)] * 2],
        "row_grads",
        [pltpu.VMEM((4, 2, 32, WIDTH), BF16)],
    )

    half = query_parts[0].astype(F32)
    for s in (1, 3, 2):
        half = half + shifted(query_parts[s], "y", s).astype(F32)
    query_sum = half[0] + shifted(half[1].astype(BF16), "zh", 1).astype(F32)
    query_grad = query_sum.astype(BF16)[None]
    kv_sum = (kv_keep + shifted(kv_send, "qi", 1)).astype(BF16)
    key_grad = kv_sum[None, :, :WIDTH]
    value_grad = kv_sum[None, :, WIDTH:]

    weight_rows = CHUNK_ROWS * CHUNKS
    weights, updated_grad = call(
        weight_kernel,
        [
            *vmem(received, *params[3:], half),
            *[in_hbm(v) for v in states[:7]],
        ],
        [
            (HBM, pltpu.HBM((weight_rows, PAIR), BF16)),
            (HBM, pltpu.HBM((cells, PAIR), F32)),
        ],
        "pair_weights",
        [
            pltpu.VMEM((128, 128), F32),
            pltpu.VMEM((weight_rows, PAIR), BF16),
            pltpu.VMEM((cells, PAIR), F32),
            *[pltpu.VMEM(v.shape, v.dtype) for v in states[:7]],
            pltpu.SemaphoreType.DMA((7,)),
            pltpu.SemaphoreType.DMA((5,)),
        ],
    )
    parts = all_to_all(weights.reshape(CHUNKS, CHUNK_ROWS, PAIR), PLANE)
    (shares,) = call(
        sum_kernel,
        vmem(parts),
        [bf16_kept(8, CHUNK_ROWS, PAIR)],
        "plane_sum",
    )
    columns = all_to_all(shares, COLUMN)
    (totals,) = call(
        sum_kernel, vmem(columns), [bf16_kept(CHUNKS, CHUNK_ROWS, PAIR)], "column_sum"
    )
    (pair_low,) = call(
        inputs_kernel,
        [
            (SMEM, place), in_hbm(totals), in_hbm(pair_rep),
            *kept(updated_grad, *states[2:4], *params[:4]),
        ],
        [bf16_kept(SUB, 2, 32, PAIR)],
        "pair_inputs",
        [pltpu.VMEM((SUB, 2, 32, PAIR), BF16), pltpu.SemaphoreType.DMA((1,))],
    )
    pair_grad = pair_low[None, None]
    table = all_to_all(totals, PLANE).reshape(weight_rows, PAIR)
    gate_grad, up_grad, down_grad, head_grad, first_grad, second_grad = call(
        unpack_kernel,
        vmem(table, *params[:3], *params[4:]),
        [
            f32_kept(PAIR, FF), f32_kept(PAIR, FF), f32_kept(FF, PAIR),
            f32_kept(HEADS, PAIR), f32_kept(1, PAIR), f32_kept(1, PAIR),
        ],
        "unpack",
    )
    return (
        query_grad, key_grad, value_grad, pair_grad, gate_grad, up_grad, down_grad,
        head_grad.T, first_grad[0], second_grad[0],
    )


def solution(mesh):
    fine = Mesh(mesh.devices.reshape(4, 4, 2, 2, 4), ("zl", "x", "qi", "zh", "y"))
    kj = ("zh", "y")
    return jax.shard_map(
        local,
        mesh=fine,
        in_specs=(
            P("qi", None, kj, None),
            P(NOISE, "qi", None),
            P(NOISE, None, kj, None),
            P(NOISE, None, kj, None),
            P(NOISE, "qi", None),
            P(),
            P(),
            P(),
            P(),
            P(),
            P(),
        ),
        out_specs=(
            P(NOISE, ("qi", "zh", "y"), None),
            P(NOISE, ("qi", "zh", "y"), None),
            P(NOISE, ("qi", "zh", "y"), None),
            P("qi", NOISE, None, None, kj, None),
            P(),
            P(),
            P(),
            P(),
            P(),
            P(),
        ),
        check_vma=False,
    )
```

```python
import functools

import jax
import jax.numpy as jnp
from jax import lax
from jax.experimental import pallas as pl
from jax.experimental.pallas import tpu as pltpu
from jax.sharding import Mesh, PartitionSpec as P

HEADS = 16
HEAD_DIM = 48
WIDTH = HEADS * HEAD_DIM
PAIR = 128
FF = 512
KEYS = 64
ROWS = 256
SUB = 16
EPSILON = 1e-05
SCALE = HEAD_DIM**-0.5
CHUNK_ROWS = 56
CHUNKS = 32
GROUP = 2
F32 = jnp.float32
BF16 = jnp.bfloat16
NOISE = ("zl", "x")
PLANE = ("qi", "x", "y")
COLUMN = ("zl", "zh")

VMEM = pl.BlockSpec(memory_space=pltpu.VMEM)
SMEM = pl.BlockSpec(memory_space=pltpu.SMEM)
HBM = pl.BlockSpec(memory_space=pltpu.HBM)
BLOCK = pl.BlockSpec()
PARAMS = pltpu.CompilerParams(vmem_limit_bytes=48 * 1024 * 1024)


def dot(left, right, dims):
    return lax.dot_general(left, right, (dims, ((), ())), preferred_element_type=F32)


NN = ((1,), (0,))
NT = ((1,), (1,))
TN = ((0,), (0,))


def layer_norm(values):
    center = values - jnp.mean(values, axis=1, keepdims=True)
    inverse = lax.rsqrt(jnp.mean(center * center, axis=1, keepdims=True) + EPSILON)
    return center * inverse, inverse


def centering_matrix():
    row = lax.broadcasted_iota(jnp.int32, (PAIR, PAIR), 0)
    column = lax.broadcasted_iota(jnp.int32, (PAIR, PAIR), 1)
    return (jnp.where(row == column, 1.0, 0.0) - 1.0 / PAIR).astype(BF16)


def centered_norm(cells, centering):
    center = dot(cells, centering, NN)
    inverse = lax.rsqrt(jnp.mean(center * center, axis=1, keepdims=True) + EPSILON)
    return center * inverse, inverse


def norm_backward(grad, normed, inverse):
    first = jnp.mean(grad, axis=1, keepdims=True)
    second = jnp.mean(grad * normed, axis=1, keepdims=True)
    return inverse * (grad - first - normed * second)


def block_cells(read_row):
    slabs = [read_row(half * 8 + step) for step in range(8) for half in range(2)]
    return jnp.concatenate(slabs, axis=0)


def silu_parts(half):
    curve = jnp.tanh(half)
    return half + half * curve, 0.5 + 0.5 * curve


def fetch(sources, targets, sems):
    copies = [
        pltpu.make_async_copy(source, target, sems.at[k])
        for k, (source, target) in enumerate(zip(sources, targets))
    ]
    for copy in copies:
        copy.start()
    return copies


def bias_kernel(
    place, pair, gain1_h, gate_h, up_h, down_h, gain2_h, head_h, out,
    cells_v, gain1, gate_w, up_w, down_w, gain2, head_t, rows, sems,
):
    x = place[1]
    blocks = [pair.at[pl.ds((zl * 4 + x) * SUB, SUB)] for zl in range(4)]
    copies = fetch(
        (*blocks, gain1_h, gate_h, up_h, down_h, gain2_h, head_h),
        (
            cells_v.at[0], cells_v.at[1], cells_v.at[2], cells_v.at[3],
            gain1, gate_w, up_w, down_w, gain2, head_t,
        ),
        sems,
    )
    for copy in copies:
        copy.wait()
    centering = centering_matrix()
    groups = [range(start, start + GROUP) for start in range(0, 4, GROUP)]

    def normed_cells(blocks):
        cells = jnp.concatenate(
            [block_cells(lambda r: cells_v[k, r].reshape(KEYS, PAIR)) for k in blocks], axis=0
        )
        return cells.astype(F32), centered_norm(cells, centering)[0]

    def project(cells, normed):
        lowered = (normed * gain1[...]).astype(BF16)
        return cells, dot(lowered, gate_w[...] * 0.5, NN), dot(lowered, up_w[...], NN)

    def activate(cells, half, up):
        return cells, (silu_parts(half)[0] * up).astype(BF16)

    def update(cells, hidden):
        return (cells + dot(hidden, down_w[...], NN),)

    def lower(updated):
        return ((layer_norm(updated)[0] * gain2[...]).astype(BF16),)

    stages = (project, activate, update, lower)
    held = [None] * len(groups)
    for step in range(len(groups) + len(stages)):
        for index, blocks in enumerate(groups):
            stage = step - index
            if stage == 0:
                held[index] = normed_cells(blocks)
            elif 0 < stage <= len(stages):
                held[index] = stages[stage - 1](*held[index])
            if stage == len(stages):
                bias = dot(head_t[...], held[index][0], NT)
                for order, k in enumerate(blocks):
                    for row in range(8):
                        lane = order * 1024 + row * 128
                        rows[k, pl.ds(row, HEADS, stride=8), :] = bias[:, lane : lane + 128]
                    out[k] = rows[k].astype(BF16)


def head_mask(shape, head):
    column = lax.broadcasted_iota(jnp.int32, shape, 1)
    return (column >= head * HEAD_DIM) & (column < (head + 1) * HEAD_DIM)


def spread_heads(tile):
    wide = tile.astype(F32)
    parts = [
        jnp.where(head_mask(wide.shape, h), wide, 0.0).astype(BF16) for h in range(HEADS)
    ]
    return jnp.concatenate(parts, axis=0)


def permute_rows(tile):
    width = tile.shape[1]
    wide = tile.astype(F32).reshape(16, 2, 8, width)
    parts = [wide[:, half].reshape(128, width) for half in range(2)]
    return jnp.concatenate(parts, axis=0).astype(BF16)


def product_kernel(query, grad, keys, values, scores, attend, query_out, grad_out, keys_out):
    query_p = permute_rows(query[...])
    grad_p = permute_rows(grad[...])
    query_out[...] = query_p
    grad_out[...] = grad_p
    wide_keys = spread_heads(keys[...].reshape(KEYS, WIDTH))
    keys_out[...] = wide_keys
    scores[...] = dot(wide_keys, query_p, NT) * SCALE
    wide_values = spread_heads(values[...].reshape(KEYS, WIDTH))
    attend[...] = dot(wide_values, grad_p, NT)


def stats_kernel(place, scores, attend, own, first, second, third, total_out, stats, wide):
    x = place[1]
    for shift, piece in enumerate((own, first, second, third)):
        origin = lax.rem(x + 4 - shift, 4)
        for zl in range(4):
            wide[zl, origin] = piece[zl].astype(F32)
    logs, means = [], []
    for h in range(HEADS):
        block = wide[:, :, 8 * h : 8 * h + 8, :].reshape(128, 128).T
        bias = jnp.concatenate([block[:KEYS], block[KEYS:]], axis=1)
        rows = slice(h * KEYS, (h + 1) * KEYS)
        total = scores[rows, :] + bias
        total_out[rows, :] = total
        largest = jnp.max(total, axis=0, keepdims=True)
        powers = jnp.exp(total - largest)
        amount = jnp.sum(powers, axis=0, keepdims=True)
        weighted = jnp.sum(powers * attend[rows, :], axis=0, keepdims=True)
        logs.append(largest + jnp.log(amount))
        means.append(weighted / amount)
    stats[...] = jnp.concatenate(logs + means, axis=0)


def merge_stats(parts):
    largest = functools.reduce(jnp.maximum, [p[:HEADS] for p in parts])
    powers = [jnp.exp(p[:HEADS] - largest) for p in parts]
    amount = functools.reduce(jnp.add, powers)
    weighted = functools.reduce(jnp.add, [p[HEADS:] * w for p, w in zip(parts, powers)])
    return largest + jnp.log(amount), weighted / amount


def merge_kernel(own, received, after, merged):
    level, delta = merge_stats([own[...], received[...]])
    merged[:HEADS, :] = level
    merged[HEADS:, :] = delta


def grad_kernel(own, first, second, third, total, attend, send, score_low, attend_low):
    level, delta = merge_stats([own[...], first[...], second[...], third[...]])
    for pair in range(HEADS // 2):
        blocks = []
        for h in (2 * pair, 2 * pair + 1):
            rows = slice(h * KEYS, (h + 1) * KEYS)
            weights = jnp.exp(total[rows, :] - level[h : h + 1])
            score = weights * (attend[rows, :] - delta[h : h + 1])
            score_low[rows, :] = score.astype(BF16)
            attend_low[rows, :] = weights.astype(BF16)
            block = jnp.concatenate([score[:, :128], score[:, 128:]], axis=0).T
            blocks.append(block.reshape(16, 8, 128))
        send[:, 16 * pair : 16 * pair + 16, :] = jnp.concatenate(blocks, axis=1).astype(BF16)


def rows_kernel(
    place, score_low, attend_low, query, grad, keys,
    query_0, query_1, query_2, query_3, kv_keep, kv_send, sends,
):
    y, zh, qi = place[2], place[3], place[4]
    product = dot(score_low[...], keys[...], TN) * SCALE
    for target in range(8):
        rel_z = lax.rem(target // 4 + zh, 2)
        rel_y = lax.rem(target % 4 + 4 - y, 4)
        parts = []
        for block in (2 * target, 2 * target + 1):
            for half in range(2):
                start = half * 128 + block * 8
                parts.append(product[start : start + 8])
        sends[rel_y, rel_z] = jnp.concatenate(parts, axis=0).astype(BF16)
    for shift, out in enumerate((query_0, query_1, query_2, query_3)):
        out[...] = sends[shift]
    for which, (low, rows) in enumerate(((score_low, query), (attend_low, grad))):
        result = jnp.zeros((KEYS, WIDTH), F32)
        for quad in range(4):
            part = dot(low[quad * 256 : quad * 256 + 256, :], rows[...], NN)
            for step in range(4):
                piece = part[step * KEYS : (step + 1) * KEYS]
                mask = head_mask(piece.shape, quad * 4 + step)
                result = result + jnp.where(mask, piece, 0.0)
        if which == 0:
            result = result * SCALE
        lanes = slice(which * WIDTH, (which + 1) * WIDTH)
        first, second = result[:32], result[32:]
        kv_keep[:, lanes] = jnp.where(qi == 0, first, second)
        kv_send[:, lanes] = jnp.where(qi == 0, second, first)


def state_kernel(
    place, after, pair, gain1, gate_w, up_w, down_w, gain2, head_t,
    post_normed_s, post_inverse_s, gate_slope, up_slope, pre_t, hidden_s, post_low,
    cells_v, sems,
):
    for copy in fetch((pair.at[pl.ds(place[0] * SUB, SUB)],), (cells_v,), sems):
        copy.wait()
    low_cells = block_cells(lambda r: cells_v[r].reshape(KEYS, PAIR))
    cells = low_cells.astype(F32)
    normed, _ = centered_norm(low_cells, centering_matrix())
    scaled = normed * gain1[...]
    pre_t[...] = scaled.T.astype(BF16)
    lowered = scaled.astype(BF16)
    half = dot(lowered, gate_w[...] * 0.5, NN)
    up = dot(lowered, up_w[...], NN)
    silu, sigmoid = silu_parts(half)
    hidden = (silu * up).astype(BF16)
    hidden_s[...] = hidden
    up_slope[...] = silu.astype(BF16)
    gate_slope[...] = (up * (sigmoid + silu * (1.0 - sigmoid))).astype(BF16)
    updated = cells + dot(hidden, down_w[...], NN)
    normed, inverse = layer_norm(updated)
    post_normed_s[...] = normed
    post_inverse_s[...] = jnp.broadcast_to(inverse, normed.shape)
    post_low[...] = (normed * gain2[...]).astype(BF16)


def weight_kernel(
    received, down_w, gain2, head_t, after, h0, h1, h2, h3, h4, h5, h6,
    weights, updated_out, rows, weights_v, updated_v,
    post_normed, post_inverse, gate_slope, up_slope, pre_t, hidden, post_low, sems, out_sems,
):
    held = (post_normed, post_inverse, gate_slope, up_slope, pre_t, hidden, post_low)
    copies = fetch((h0, h1, h2, h3, h4, h5, h6), held, sems)
    rows[...] = jnp.sum(received[...].astype(F32), axis=0)
    low = jnp.concatenate(
        [rows[pl.ds(step, HEADS, stride=8), :] for step in range(8)], axis=1
    ).astype(BF16)
    spans = [slice(start, start + 512) for start in (0, 512)]
    post_scaled = [dot(low[:, span], head_t[...], TN) for span in spans]
    copies[0].wait()
    copies[1].wait()
    updated_grads = [
        norm_backward(scaled * gain2[...], post_normed[span, :], post_inverse[span, :])
        for scaled, span in zip(post_scaled, spans)
    ]
    for grad, span in zip(updated_grads, spans):
        updated_v[span, :] = grad
    outs = fetch((updated_v,), (updated_out,), out_sems)
    updated_lows = [grad.astype(BF16) for grad in updated_grads]
    hidden_grads = [dot(grad, down_w[...], NT) for grad in updated_lows]
    for copy in copies[2:]:
        copy.wait()
    gate_low = jnp.concatenate(
        [(g * gate_slope[span, :]).astype(BF16) for g, span in zip(hidden_grads, spans)], axis=0
    )
    up_low = jnp.concatenate(
        [(g * up_slope[span, :]).astype(BF16) for g, span in zip(hidden_grads, spans)], axis=0
    )
    updated_low = jnp.concatenate(updated_lows, axis=0)

    def give(first, rows_of, k):
        part = pl.ds(first, rows_of)
        outs.extend(fetch((weights_v.at[part],), (weights.at[part],), out_sems.at[pl.ds(k, 1)]))

    def place_part(first, part, k):
        for block in range(4):
            lanes = slice(block * 128, (block + 1) * 128)
            weights_v[first + block * 128 : first + (block + 1) * 128, :] = part[:, lanes]
        give(first, 512, k)

    rest = CHUNKS * CHUNK_ROWS - 1536
    weights_v[1536:1552, :] = dot(low, post_low[...], NN).astype(BF16)
    weights_v[1552:, :] = jnp.zeros((rest - 16, PAIR), BF16)
    give(1536, rest, 1)
    place_part(1024, dot(updated_low, hidden[...], TN).astype(BF16), 2)
    place_part(0, dot(pre_t[...], gate_low, NN).astype(BF16), 3)
    place_part(512, dot(pre_t[...], up_low, NN).astype(BF16), 4)
    for copy in outs:
        copy.wait()


def inputs_kernel(
    place, after, pair, updated_grad, gate_slope, up_slope, gain1, gate_w, up_w, down_w,
    pair_out, cells_v, sems,
):
    copies = fetch((pair.at[pl.ds(place[0] * SUB, SUB)],), (cells_v,), sems)
    hidden_grad = dot(updated_grad[...].astype(BF16), down_w[...], NT)
    gate_low = (hidden_grad * gate_slope[...]).astype(BF16)
    up_low = (hidden_grad * up_slope[...]).astype(BF16)
    pre_scaled = dot(gate_low, gate_w[...], NT) + dot(up_low, up_w[...], NT)
    for copy in copies:
        copy.wait()
    cells = block_cells(lambda r: cells_v[r].reshape(KEYS, PAIR)).astype(F32)
    inputs_grad = norm_backward(pre_scaled * gain1[...], *layer_norm(cells))
    result = (updated_grad[...] + inputs_grad).astype(BF16)
    for step in range(8):
        for half in range(2):
            start = step * 128 + half * KEYS
            slab = result[start : start + KEYS]
            pair_out[half * 8 + step] = slab.reshape(2, 32, PAIR)


def sum_kernel(parts, out):
    total = jnp.sum(parts[...].astype(F32), axis=0).astype(out.dtype)
    for j in range(out.shape[0]):
        out[j] = total


def unpack_kernel(
    table, gain1, gate_w, up_w, gain2, head_t,
    gate_out, up_out, down_out, head_out, first_out, second_out,
):
    factor = 1.0 / 512

    def block(k):
        return table[k * 128 : (k + 1) * 128, :].astype(F32) * factor

    total = jnp.zeros((PAIR, 128), F32)
    for k in range(4):
        lanes = slice(k * 128, (k + 1) * 128)
        gate, up = block(k), block(4 + k)
        gate_out[:, lanes] = gate
        up_out[:, lanes] = up
        down_out[lanes, :] = block(8 + k).T
        total = total + gate * gate_w[:, lanes].astype(F32) + up * up_w[:, lanes].astype(F32)
    head = block(12)[:HEADS]
    head_out[...] = head
    first_out[...] = jnp.sum(total.T, axis=0, keepdims=True) / gain1[...]
    second = jnp.sum(head * head_t[...].astype(F32), axis=0, keepdims=True)
    second_out[...] = second / gain2[...]


def shifted(value, axis, shift):
    size = lax.axis_size(axis)
    return lax.ppermute(value, axis, [(i, (i + shift) % size) for i in range(size)])


def all_to_all(value, axes):
    return lax.all_to_all(value, axes, 0, 0, tiled=True)


def local(
    pair_rep, query_rows, key_rows, value_rows, output_grad,
    gain_first, gate_weight, up_weight, down_weight, gain_second, head_weight,
):
    x, zl = lax.axis_index("x"), lax.axis_index("zl")
    y, zh, qi = lax.axis_index("y"), lax.axis_index("zh"), lax.axis_index("qi")
    place = jnp.stack([zl * 4 + x, x, y, zh, qi]).astype(jnp.int32)
    params = (
        gain_first[None], gate_weight, up_weight, down_weight, gain_second[None], head_weight.T,
    )

    def call(kernel, ins, outs, name, scratch=()):
        return pl.pallas_call(
            kernel,
            in_specs=[spec for spec, _ in ins],
            out_specs=[spec for spec, _ in outs],
            out_shape=[out for _, out in outs],
            scratch_shapes=list(scratch),
            compiler_params=PARAMS,
            name=name,
        )(*[value for _, value in ins])

    def vmem(*values):
        return [(VMEM, value) for value in values]

    def kept(*values):
        return [(BLOCK, pltpu.with_memory_space_constraint(v, pltpu.HBM)) for v in values]

    def f32(*dims):
        return (VMEM, jax.ShapeDtypeStruct(dims, F32))

    def bf16(*dims):
        return (VMEM, jax.ShapeDtypeStruct(dims, BF16))

    def f32_kept(*dims):
        return (BLOCK, pltpu.HBM(dims, F32))

    def bf16_kept(*dims):
        return (BLOCK, pltpu.HBM(dims, BF16))

    def in_hbm(value):
        return (HBM, pltpu.with_memory_space_constraint(value, pltpu.HBM))

    (own,) = call(
        bias_kernel,
        [(SMEM, place), in_hbm(pair_rep), *[in_hbm(p) for p in params]],
        [bf16(4, 128, 128)],
        "pair_bias",
        [
            pltpu.VMEM((4, SUB, 2, 32, PAIR), BF16),
            *[pltpu.VMEM(p.shape, p.dtype) for p in params],
            pltpu.VMEM((4, 128, 128), F32),
            pltpu.SemaphoreType.DMA((10,)),
        ],
    )
    first, third, second = [shifted(own, "x", s) for s in (1, 3, 2)]

    scores, attend, query_p, grad_p, wide_keys = call(
        product_kernel,
        vmem(query_rows[0], output_grad[0], key_rows[0], value_rows[0]),
        [
            f32(HEADS * KEYS, ROWS), f32(HEADS * KEYS, ROWS), bf16_kept(ROWS, WIDTH),
            bf16_kept(ROWS, WIDTH), bf16_kept(HEADS * KEYS, WIDTH),
        ],
        "products",
    )

    total, stats = call(
        stats_kernel,
        [(SMEM, place), *vmem(scores, attend, own, first, second, third)],
        [f32(HEADS * KEYS, ROWS), f32(2 * HEADS, ROWS)],
        "softmax_stats",
        [pltpu.VMEM((4, 4, 128, 128), F32)],
    )

    cells = SUB * KEYS
    states = call(
        state_kernel,
        [(SMEM, place), *vmem(total), in_hbm(pair_rep), *vmem(*params)],
        [
            f32_kept(cells, PAIR), f32_kept(cells, PAIR), bf16_kept(cells, FF),
            bf16_kept(cells, FF), bf16_kept(PAIR, cells), bf16_kept(cells, FF),
            bf16_kept(cells, PAIR),
        ],
        "pair_states",
        [pltpu.VMEM((SUB, 2, 32, PAIR), BF16), pltpu.SemaphoreType.DMA((1,))],
    )

    (merged,) = call(
        merge_kernel,
        [*vmem(stats, shifted(stats, "zh", 1)), in_hbm(states[0])],
        [f32(2 * HEADS, ROWS)],
        "merge_stats",
    )
    peers = [shifted(merged, "y", s) for s in (1, 3, 2)]

    send, score_low, attend_low = call(
        grad_kernel,
        vmem(merged, *peers, total, attend),
        [bf16_kept(16, 128, 128), *[bf16_kept(HEADS * KEYS, ROWS)] * 2],
        "score_grads",
    )

    received = all_to_all(send, NOISE)

    *query_parts, kv_keep, kv_send = call(
        rows_kernel,
        [(SMEM, place), *kept(score_low, attend_low, query_p, grad_p, wide_keys)],
        [*[bf16(2, 32, WIDTH)] * 4, *[f32(32, 2 * WIDTH)] * 2],
        "row_grads",
        [pltpu.VMEM((4, 2, 32, WIDTH), BF16)],
    )

    half = query_parts[0].astype(F32)
    for s in (1, 3, 2):
        half = half + shifted(query_parts[s], "y", s).astype(F32)
    query_sum = half[0] + shifted(half[1].astype(BF16), "zh", 1).astype(F32)
    query_grad = query_sum.astype(BF16)[None]
    kv_sum = (kv_keep + shifted(kv_send, "qi", 1)).astype(BF16)
    key_grad = kv_sum[None, :, :WIDTH]
    value_grad = kv_sum[None, :, WIDTH:]

    weight_rows = CHUNK_ROWS * CHUNKS
    weights, updated_grad = call(
        weight_kernel,
        [
            *vmem(received, *params[3:], half),
            *[in_hbm(v) for v in states[:7]],
        ],
        [
            (HBM, pltpu.HBM((weight_rows, PAIR), BF16)),
            (HBM, pltpu.HBM((cells, PAIR), F32)),
        ],
        "pair_weights",
        [
            pltpu.VMEM((128, 128), F32),
            pltpu.VMEM((weight_rows, PAIR), BF16),
            pltpu.VMEM((cells, PAIR), F32),
            *[pltpu.VMEM(v.shape, v.dtype) for v in states[:7]],
            pltpu.SemaphoreType.DMA((7,)),
            pltpu.SemaphoreType.DMA((5,)),
        ],
    )
    parts = all_to_all(weights.reshape(CHUNKS, CHUNK_ROWS, PAIR), PLANE)
    (shares,) = call(
        sum_kernel,
        vmem(parts),
        [bf16_kept(8, CHUNK_ROWS, PAIR)],
        "plane_sum",
    )
    columns = all_to_all(shares, COLUMN)
    (totals,) = call(
        sum_kernel, vmem(columns), [bf16_kept(CHUNKS, CHUNK_ROWS, PAIR)], "column_sum"
    )
    (pair_low,) = call(
        inputs_kernel,
        [
            (SMEM, place), in_hbm(totals), in_hbm(pair_rep),
            *kept(updated_grad, *states[2:4], *params[:4]),
        ],
        [bf16_kept(SUB, 2, 32, PAIR)],
        "pair_inputs",
        [pltpu.VMEM((SUB, 2, 32, PAIR), BF16), pltpu.SemaphoreType.DMA((1,))],
    )
    pair_grad = pair_low[None, None]
    table = all_to_all(totals, PLANE).reshape(weight_rows, PAIR)
    gate_grad, up_grad, down_grad, head_grad, first_grad, second_grad = call(
        unpack_kernel,
        vmem(table, *params[:3], *params[4:]),
        [
            f32_kept(PAIR, FF), f32_kept(PAIR, FF), f32_kept(FF, PAIR),
            f32_kept(HEADS, PAIR), f32_kept(1, PAIR), f32_kept(1, PAIR),
        ],
        "unpack",
    )
    return (
        query_grad, key_grad, value_grad, pair_grad, gate_grad, up_grad, down_grad,
        head_grad.T, first_grad[0], second_grad[0],
    )


def solution(mesh):
    fine = Mesh(mesh.devices.reshape(4, 4, 2, 2, 4), ("zl", "x", "qi", "zh", "y"))
    kj = ("zh", "y")
    return jax.shard_map(
        local,
        mesh=fine,
        in_specs=(
            P("qi", None, kj, None),
            P(NOISE, "qi", None),
            P(NOISE, None, kj, None),
            P(NOISE, None, kj, None),
            P(NOISE, "qi", None),
            P(),
            P(),
            P(),
            P(),
            P(),
            P(),
        ),
        out_specs=(
            P(NOISE, ("qi", "zh", "y"), None),
            P(NOISE, ("qi", "zh", "y"), None),
            P(NOISE, ("qi", "zh", "y"), None),
            P("qi", NOISE, None, None, kj, None),
            P(),
            P(),
            P(),
            P(),
            P(),
            P(),
        ),
        check_vma=False,
    )
```

```python
import functools

import jax
import jax.numpy as jnp
from jax import lax
from jax.experimental import pallas as pl
from jax.experimental.pallas import tpu as pltpu
from jax.sharding import Mesh, PartitionSpec as P

HEADS = 16
HEAD_DIM = 48
WIDTH = HEADS * HEAD_DIM
PAIR = 128
FF = 512
KEYS = 64
ROWS = 256
SUB = 16
EPSILON = 1e-05
SCALE = HEAD_DIM**-0.5
CHUNK_ROWS = 56
CHUNKS = 32
GROUP = 2
F32 = jnp.float32
BF16 = jnp.bfloat16
NOISE = ("zl", "x")
PLANE = ("qi", "x", "y")
COLUMN = ("zl", "zh")

VMEM = pl.BlockSpec(memory_space=pltpu.VMEM)
SMEM = pl.BlockSpec(memory_space=pltpu.SMEM)
HBM = pl.BlockSpec(memory_space=pltpu.HBM)
BLOCK = pl.BlockSpec()
PARAMS = pltpu.CompilerParams(vmem_limit_bytes=48 * 1024 * 1024)


def dot(left, right, dims):
    return lax.dot_general(left, right, (dims, ((), ())), preferred_element_type=F32)


NN = ((1,), (0,))
NT = ((1,), (1,))
TN = ((0,), (0,))


def layer_norm(values):
    center = values - jnp.mean(values, axis=1, keepdims=True)
    inverse = lax.rsqrt(jnp.mean(center * center, axis=1, keepdims=True) + EPSILON)
    return center * inverse, inverse


def centering_matrix():
    row = lax.broadcasted_iota(jnp.int32, (PAIR, PAIR), 0)
    column = lax.broadcasted_iota(jnp.int32, (PAIR, PAIR), 1)
    return (jnp.where(row == column, 1.0, 0.0) - 1.0 / PAIR).astype(BF16)


def centered_norm(cells, centering):
    center = dot(cells, centering, NN)
    inverse = lax.rsqrt(jnp.mean(center * center, axis=1, keepdims=True) + EPSILON)
    return center * inverse, inverse


def norm_backward(grad, normed, inverse):
    first = jnp.mean(grad, axis=1, keepdims=True)
    second = jnp.mean(grad * normed, axis=1, keepdims=True)
    return inverse * (grad - first - normed * second)


def block_cells(read_row):
    slabs = [read_row(half * 8 + step) for step in range(8) for half in range(2)]
    return jnp.concatenate(slabs, axis=0)


def silu_parts(half):
    curve = jnp.tanh(half)
    return half + half * curve, 0.5 + 0.5 * curve


def fetch(sources, targets, sems):
    copies = [
        pltpu.make_async_copy(source, target, sems.at[k])
        for k, (source, target) in enumerate(zip(sources, targets))
    ]
    for copy in copies:
        copy.start()
    return copies


def bias_kernel(
    place, pair, gain1_h, gate_h, up_h, down_h, gain2_h, head_h, out,
    cells_v, gain1, gate_w, up_w, down_w, gain2, head_t, rows, sems,
):
    x = place[1]
    blocks = [pair.at[pl.ds((zl * 4 + x) * SUB, SUB)] for zl in range(4)]
    copies = fetch(
        (*blocks, gain1_h, gate_h, up_h, down_h, gain2_h, head_h),
        (
            cells_v.at[0], cells_v.at[1], cells_v.at[2], cells_v.at[3],
            gain1, gate_w, up_w, down_w, gain2, head_t,
        ),
        sems,
    )
    for copy in copies:
        copy.wait()
    centering = centering_matrix()
    groups = [range(start, start + GROUP) for start in range(0, 4, GROUP)]

    def normed_cells(blocks):
        cells = jnp.concatenate(
            [block_cells(lambda r: cells_v[k, r].reshape(KEYS, PAIR)) for k in blocks], axis=0
        )
        return cells.astype(F32), centered_norm(cells, centering)[0]

    def project(cells, normed):
        lowered = (normed * gain1[...]).astype(BF16)
        return cells, dot(lowered, gate_w[...] * 0.5, NN), dot(lowered, up_w[...], NN)

    def activate(cells, half, up):
        return cells, (silu_parts(half)[0] * up).astype(BF16)

    def update(cells, hidden):
        return (cells + dot(hidden, down_w[...], NN),)

    def lower(updated):
        return ((layer_norm(updated)[0] * gain2[...]).astype(BF16),)

    stages = (project, activate, update, lower)
    held = [None] * len(groups)
    for step in range(len(groups) + len(stages)):
        for index, blocks in enumerate(groups):
            stage = step - index
            if stage == 0:
                held[index] = normed_cells(blocks)
            elif 0 < stage <= len(stages):
                held[index] = stages[stage - 1](*held[index])
            if stage == len(stages):
                bias = dot(head_t[...], held[index][0], NT)
                for order, k in enumerate(blocks):
                    for row in range(8):
                        lane = order * 1024 + row * 128
                        rows[k, pl.ds(row, HEADS, stride=8), :] = bias[:, lane : lane + 128]
                    out[k] = rows[k].astype(BF16)


def head_mask(shape, head):
    column = lax.broadcasted_iota(jnp.int32, shape, 1)
    return (column >= head * HEAD_DIM) & (column < (head + 1) * HEAD_DIM)


def spread_heads(tile):
    wide = tile.astype(F32)
    parts = [
        jnp.where(head_mask(wide.shape, h), wide, 0.0).astype(BF16) for h in range(HEADS)
    ]
    return jnp.concatenate(parts, axis=0)


def permute_rows(tile):
    width = tile.shape[1]
    wide = tile.astype(F32).reshape(16, 2, 8, width)
    parts = [wide[:, half].reshape(128, width) for half in range(2)]
    return jnp.concatenate(parts, axis=0).astype(BF16)


def product_kernel(query, grad, keys, values, scores, attend, query_out, grad_out, keys_out):
    query_p = permute_rows(query[...])
    grad_p = permute_rows(grad[...])
    query_out[...] = query_p
    grad_out[...] = grad_p
    wide_keys = spread_heads(keys[...].reshape(KEYS, WIDTH))
    keys_out[...] = wide_keys
    scores[...] = dot(wide_keys, query_p, NT) * SCALE
    wide_values = spread_heads(values[...].reshape(KEYS, WIDTH))
    attend[...] = dot(wide_values, grad_p, NT)


def stats_kernel(place, scores, attend, own, first, second, third, total_out, stats, wide):
    x = place[1]
    for shift, piece in enumerate((own, first, second, third)):
        origin = lax.rem(x + 4 - shift, 4)
        for zl in range(4):
            wide[zl, origin] = piece[zl].astype(F32)
    logs, means = [], []
    for h in range(HEADS):
        block = wide[:, :, 8 * h : 8 * h + 8, :].reshape(128, 128).T
        bias = jnp.concatenate([block[:KEYS], block[KEYS:]], axis=1)
        rows = slice(h * KEYS, (h + 1) * KEYS)
        total = scores[rows, :] + bias
        total_out[rows, :] = total
        largest = jnp.max(total, axis=0, keepdims=True)
        powers = jnp.exp(total - largest)
        amount = jnp.sum(powers, axis=0, keepdims=True)
        weighted = jnp.sum(powers * attend[rows, :], axis=0, keepdims=True)
        logs.append(largest + jnp.log(amount))
        means.append(weighted / amount)
    stats[...] = jnp.concatenate(logs + means, axis=0)


def merge_stats(parts):
    largest = functools.reduce(jnp.maximum, [p[:HEADS] for p in parts])
    powers = [jnp.exp(p[:HEADS] - largest) for p in parts]
    amount = functools.reduce(jnp.add, powers)
    weighted = functools.reduce(jnp.add, [p[HEADS:] * w for p, w in zip(parts, powers)])
    return largest + jnp.log(amount), weighted / amount


def merge_kernel(own, received, after, merged):
    level, delta = merge_stats([own[...], received[...]])
    merged[:HEADS, :] = level
    merged[HEADS:, :] = delta


def grad_kernel(own, first, second, third, total, attend, send, score_low, attend_low):
    level, delta = merge_stats([own[...], first[...], second[...], third[...]])
    for pair in range(HEADS // 2):
        blocks = []
        for h in (2 * pair, 2 * pair + 1):
            rows = slice(h * KEYS, (h + 1) * KEYS)
            weights = jnp.exp(total[rows, :] - level[h : h + 1])
            score = weights * (attend[rows, :] - delta[h : h + 1])
            score_low[rows, :] = score.astype(BF16)
            attend_low[rows, :] = weights.astype(BF16)
            block = jnp.concatenate([score[:, :128], score[:, 128:]], axis=0).T
            blocks.append(block.reshape(16, 8, 128))
        send[:, 16 * pair : 16 * pair + 16, :] = jnp.concatenate(blocks, axis=1).astype(BF16)


def rows_kernel(
    place, score_low, attend_low, query, grad, keys,
    query_0, query_1, query_2, query_3, kv_keep, kv_send, sends,
):
    y, zh, qi = place[2], place[3], place[4]
    product = dot(score_low[...], keys[...], TN) * SCALE
    for target in range(8):
        rel_z = lax.rem(target // 4 + zh, 2)
        rel_y = lax.rem(target % 4 + 4 - y, 4)
        parts = []
        for block in (2 * target, 2 * target + 1):
            for half in range(2):
                start = half * 128 + block * 8
                parts.append(product[start : start + 8])
        sends[rel_y, rel_z] = jnp.concatenate(parts, axis=0).astype(BF16)
    for shift, out in enumerate((query_0, query_1, query_2, query_3)):
        out[...] = sends[shift]
    for which, (low, rows) in enumerate(((score_low, query), (attend_low, grad))):
        result = jnp.zeros((KEYS, WIDTH), F32)
        for quad in range(4):
            part = dot(low[quad * 256 : quad * 256 + 256, :], rows[...], NN)
            for step in range(4):
                piece = part[step * KEYS : (step + 1) * KEYS]
                mask = head_mask(piece.shape, quad * 4 + step)
                result = result + jnp.where(mask, piece, 0.0)
        if which == 0:
            result = result * SCALE
        lanes = slice(which * WIDTH, (which + 1) * WIDTH)
        first, second = result[:32], result[32:]
        kv_keep[:, lanes] = jnp.where(qi == 0, first, second)
        kv_send[:, lanes] = jnp.where(qi == 0, second, first)


def state_kernel(
    place, after, pair, gain1, gate_w, up_w, down_w, gain2, head_t,
    post_normed_s, post_inverse_s, gate_slope, up_slope, pre_t, hidden_s, post_low,
    cells_v, sems,
):
    for copy in fetch((pair.at[pl.ds(place[0] * SUB, SUB)],), (cells_v,), sems):
        copy.wait()
    low_cells = block_cells(lambda r: cells_v[r].reshape(KEYS, PAIR))
    cells = low_cells.astype(F32)
    normed, _ = centered_norm(low_cells, centering_matrix())
    scaled = normed * gain1[...]
    pre_t[...] = scaled.T.astype(BF16)
    lowered = scaled.astype(BF16)
    half = dot(lowered, gate_w[...] * 0.5, NN)
    up = dot(lowered, up_w[...], NN)
    silu, sigmoid = silu_parts(half)
    hidden = (silu * up).astype(BF16)
    hidden_s[...] = hidden
    up_slope[...] = silu.astype(BF16)
    gate_slope[...] = (up * (sigmoid + silu * (1.0 - sigmoid))).astype(BF16)
    updated = cells + dot(hidden, down_w[...], NN)
    normed, inverse = layer_norm(updated)
    post_normed_s[...] = normed
    post_inverse_s[...] = jnp.broadcast_to(inverse, normed.shape)
    post_low[...] = (normed * gain2[...]).astype(BF16)


def weight_kernel(
    received, down_w, gain2, head_t, after, h0, h1, h2, h3, h4, h5, h6,
    weights, updated_out, rows, weights_v, updated_v,
    post_normed, post_inverse, gate_slope, up_slope, pre_t, hidden, post_low, sems, out_sems,
):
    held = (post_normed, post_inverse, gate_slope, up_slope, pre_t, hidden, post_low)
    copies = fetch((h0, h1, h2, h3, h4, h5, h6), held, sems)
    rows[...] = jnp.sum(received[...].astype(F32), axis=0)
    low = jnp.concatenate(
        [rows[pl.ds(step, HEADS, stride=8), :] for step in range(8)], axis=1
    ).astype(BF16)
    spans = [slice(start, start + 512) for start in (0, 512)]
    post_scaled = [dot(low[:, span], head_t[...], TN) for span in spans]
    copies[0].wait()
    copies[1].wait()
    updated_grads = [
        norm_backward(scaled * gain2[...], post_normed[span, :], post_inverse[span, :])
        for scaled, span in zip(post_scaled, spans)
    ]
    for grad, span in zip(updated_grads, spans):
        updated_v[span, :] = grad
    outs = fetch((updated_v,), (updated_out,), out_sems)
    updated_lows = [grad.astype(BF16) for grad in updated_grads]
    hidden_grads = [dot(grad, down_w[...], NT) for grad in updated_lows]
    for copy in copies[2:]:
        copy.wait()
    gate_low = jnp.concatenate(
        [(g * gate_slope[span, :]).astype(BF16) for g, span in zip(hidden_grads, spans)], axis=0
    )
    up_low = jnp.concatenate(
        [(g * up_slope[span, :]).astype(BF16) for g, span in zip(hidden_grads, spans)], axis=0
    )
    updated_low = jnp.concatenate(updated_lows, axis=0)

    def give(first, rows_of, k):
        part = pl.ds(first, rows_of)
        outs.extend(fetch((weights_v.at[part],), (weights.at[part],), out_sems.at[pl.ds(k, 1)]))

    def place_part(first, part, k):
        for block in range(4):
            lanes = slice(block * 128, (block + 1) * 128)
            weights_v[first + block * 128 : first + (block + 1) * 128, :] = part[:, lanes]
        give(first, 512, k)

    rest = CHUNKS * CHUNK_ROWS - 1536
    weights_v[1536:1552, :] = dot(low, post_low[...], NN).astype(BF16)
    weights_v[1552:, :] = jnp.zeros((rest - 16, PAIR), BF16)
    give(1536, rest, 1)
    place_part(1024, dot(updated_low, hidden[...], TN).astype(BF16), 2)
    place_part(0, dot(pre_t[...], gate_low, NN).astype(BF16), 3)
    place_part(512, dot(pre_t[...], up_low, NN).astype(BF16), 4)
    for copy in outs:
        copy.wait()


def inputs_kernel(
    place, after, pair, updated_grad, gate_slope, up_slope, gain1, gate_w, up_w, down_w,
    pair_out, cells_v, sems,
):
    copies = fetch((pair.at[pl.ds(place[0] * SUB, SUB)],), (cells_v,), sems)
    hidden_grad = dot(updated_grad[...].astype(BF16), down_w[...], NT)
    gate_low = (hidden_grad * gate_slope[...]).astype(BF16)
    up_low = (hidden_grad * up_slope[...]).astype(BF16)
    pre_scaled = dot(gate_low, gate_w[...], NT) + dot(up_low, up_w[...], NT)
    for copy in copies:
        copy.wait()
    cells = block_cells(lambda r: cells_v[r].reshape(KEYS, PAIR)).astype(F32)
    inputs_grad = norm_backward(pre_scaled * gain1[...], *layer_norm(cells))
    result = (updated_grad[...] + inputs_grad).astype(BF16)
    for step in range(8):
        for half in range(2):
            start = step * 128 + half * KEYS
            slab = result[start : start + KEYS]
            pair_out[half * 8 + step] = slab.reshape(2, 32, PAIR)


def sum_kernel(parts, out):
    total = jnp.sum(parts[...].astype(F32), axis=0).astype(out.dtype)
    for j in range(out.shape[0]):
        out[j] = total


def unpack_kernel(
    table, gain1, gate_w, up_w, gain2, head_t,
    gate_out, up_out, down_out, head_out, first_out, second_out,
):
    factor = 1.0 / 512

    def block(k):
        return table[k * 128 : (k + 1) * 128, :].astype(F32) * factor

    total = jnp.zeros((PAIR, 128), F32)
    for k in range(4):
        lanes = slice(k * 128, (k + 1) * 128)
        gate, up = block(k), block(4 + k)
        gate_out[:, lanes] = gate
        up_out[:, lanes] = up
        down_out[lanes, :] = block(8 + k).T
        total = total + gate * gate_w[:, lanes].astype(F32) + up * up_w[:, lanes].astype(F32)
    head = block(12)[:HEADS]
    head_out[...] = head
    first_out[...] = jnp.sum(total.T, axis=0, keepdims=True) / gain1[...]
    second = jnp.sum(head * head_t[...].astype(F32), axis=0, keepdims=True)
    second_out[...] = second / gain2[...]


def shifted(value, axis, shift):
    size = lax.axis_size(axis)
    return lax.ppermute(value, axis, [(i, (i + shift) % size) for i in range(size)])


def all_to_all(value, axes):
    return lax.all_to_all(value, axes, 0, 0, tiled=True)


def local(
    pair_rep, query_rows, key_rows, value_rows, output_grad,
    gain_first, gate_weight, up_weight, down_weight, gain_second, head_weight,
):
    x, zl = lax.axis_index("x"), lax.axis_index("zl")
    y, zh, qi = lax.axis_index("y"), lax.axis_index("zh"), lax.axis_index("qi")
    place = jnp.stack([zl * 4 + x, x, y, zh, qi]).astype(jnp.int32)
    params = (
        gain_first[None], gate_weight, up_weight, down_weight, gain_second[None], head_weight.T,
    )

    def call(kernel, ins, outs, name, scratch=()):
        return pl.pallas_call(
            kernel,
            in_specs=[spec for spec, _ in ins],
            out_specs=[spec for spec, _ in outs],
            out_shape=[out for _, out in outs],
            scratch_shapes=list(scratch),
            compiler_params=PARAMS,
            name=name,
        )(*[value for _, value in ins])

    def vmem(*values):
        return [(VMEM, value) for value in values]

    def kept(*values):
        return [(BLOCK, pltpu.with_memory_space_constraint(v, pltpu.HBM)) for v in values]

    def f32(*dims):
        return (VMEM, jax.ShapeDtypeStruct(dims, F32))

    def bf16(*dims):
        return (VMEM, jax.ShapeDtypeStruct(dims, BF16))

    def f32_kept(*dims):
        return (BLOCK, pltpu.HBM(dims, F32))

    def bf16_kept(*dims):
        return (BLOCK, pltpu.HBM(dims, BF16))

    def in_hbm(value):
        return (HBM, pltpu.with_memory_space_constraint(value, pltpu.HBM))

    (own,) = call(
        bias_kernel,
        [(SMEM, place), in_hbm(pair_rep), *[in_hbm(p) for p in params]],
        [bf16(4, 128, 128)],
        "pair_bias",
        [
            pltpu.VMEM((4, SUB, 2, 32, PAIR), BF16),
            *[pltpu.VMEM(p.shape, p.dtype) for p in params],
            pltpu.VMEM((4, 128, 128), F32),
            pltpu.SemaphoreType.DMA((10,)),
        ],
    )
    first, third, second = [shifted(own, "x", s) for s in (1, 3, 2)]

    scores, attend, query_p, grad_p, wide_keys = call(
        product_kernel,
        vmem(query_rows[0], output_grad[0], key_rows[0], value_rows[0]),
        [
            f32(HEADS * KEYS, ROWS), f32(HEADS * KEYS, ROWS), bf16_kept(ROWS, WIDTH),
            bf16_kept(ROWS, WIDTH), bf16_kept(HEADS * KEYS, WIDTH),
        ],
        "products",
    )

    total, stats = call(
        stats_kernel,
        [(SMEM, place), *vmem(scores, attend, own, first, second, third)],
        [f32(HEADS * KEYS, ROWS), f32(2 * HEADS, ROWS)],
        "softmax_stats",
        [pltpu.VMEM((4, 4, 128, 128), F32)],
    )

    cells = SUB * KEYS
    states = call(
        state_kernel,
        [(SMEM, place), *vmem(total), in_hbm(pair_rep), *vmem(*params)],
        [
            f32_kept(cells, PAIR), f32_kept(cells, PAIR), bf16_kept(cells, FF),
            bf16_kept(cells, FF), bf16_kept(PAIR, cells), bf16_kept(cells, FF),
            bf16_kept(cells, PAIR),
        ],
        "pair_states",
        [pltpu.VMEM((SUB, 2, 32, PAIR), BF16), pltpu.SemaphoreType.DMA((1,))],
    )

    (merged,) = call(
        merge_kernel,
        [*vmem(stats, shifted(stats, "zh", 1)), in_hbm(states[0])],
        [f32(2 * HEADS, ROWS)],
        "merge_stats",
    )
    peers = [shifted(merged, "y", s) for s in (1, 3, 2)]

    send, score_low, attend_low = call(
        grad_kernel,
        vmem(merged, *peers, total, attend),
        [bf16_kept(16, 128, 128), *[bf16_kept(HEADS * KEYS, ROWS)] * 2],
        "score_grads",
    )

    received = all_to_all(send, NOISE)

    *query_parts, kv_keep, kv_send = call(
        rows_kernel,
        [(SMEM, place), *kept(score_low, attend_low, query_p, grad_p, wide_keys)],
        [*[bf16(2, 32, WIDTH)] * 4, *[f32(32, 2 * WIDTH)] * 2],
        "row_grads",
        [pltpu.VMEM((4, 2, 32, WIDTH), BF16)],
    )

    half = query_parts[0].astype(F32)
    for s in (1, 3, 2):
        half = half + shifted(query_parts[s], "y", s).astype(F32)
    query_sum = half[0] + shifted(half[1].astype(BF16), "zh", 1).astype(F32)
    query_grad = query_sum.astype(BF16)[None]
    kv_sum = (kv_keep + shifted(kv_send, "qi", 1)).astype(BF16)
    key_grad = kv_sum[None, :, :WIDTH]
    value_grad = kv_sum[None, :, WIDTH:]

    weight_rows = CHUNK_ROWS * CHUNKS
    weights, updated_grad = call(
        weight_kernel,
        [
            *vmem(received, *params[3:], query_parts[1]),
            *[in_hbm(v) for v in states[:7]],
        ],
        [
            (HBM, pltpu.HBM((weight_rows, PAIR), BF16)),
            (HBM, pltpu.HBM((cells, PAIR), F32)),
        ],
        "pair_weights",
        [
            pltpu.VMEM((128, 128), F32),
            pltpu.VMEM((weight_rows, PAIR), BF16),
            pltpu.VMEM((cells, PAIR), F32),
            *[pltpu.VMEM(v.shape, v.dtype) for v in states[:7]],
            pltpu.SemaphoreType.DMA((7,)),
            pltpu.SemaphoreType.DMA((5,)),
        ],
    )
    parts = all_to_all(weights.reshape(CHUNKS, CHUNK_ROWS, PAIR), PLANE)
    (shares,) = call(
        sum_kernel,
        vmem(parts),
        [bf16_kept(8, CHUNK_ROWS, PAIR)],
        "plane_sum",
    )
    columns = all_to_all(shares, COLUMN)
    (totals,) = call(
        sum_kernel, vmem(columns), [bf16_kept(CHUNKS, CHUNK_ROWS, PAIR)], "column_sum"
    )
    (pair_low,) = call(
        inputs_kernel,
        [
            (SMEM, place), in_hbm(totals), in_hbm(pair_rep),
            *kept(updated_grad, *states[2:4], *params[:4]),
        ],
        [bf16_kept(SUB, 2, 32, PAIR)],
        "pair_inputs",
        [pltpu.VMEM((SUB, 2, 32, PAIR), BF16), pltpu.SemaphoreType.DMA((1,))],
    )
    pair_grad = pair_low[None, None]
    table = all_to_all(totals, PLANE).reshape(weight_rows, PAIR)
    gate_grad, up_grad, down_grad, head_grad, first_grad, second_grad = call(
        unpack_kernel,
        vmem(table, *params[:3], *params[4:]),
        [
            f32_kept(PAIR, FF), f32_kept(PAIR, FF), f32_kept(FF, PAIR),
            f32_kept(HEADS, PAIR), f32_kept(1, PAIR), f32_kept(1, PAIR),
        ],
        "unpack",
    )
    return (
        query_grad, key_grad, value_grad, pair_grad, gate_grad, up_grad, down_grad,
        head_grad.T, first_grad[0], second_grad[0],
    )


def solution(mesh):
    fine = Mesh(mesh.devices.reshape(4, 4, 2, 2, 4), ("zl", "x", "qi", "zh", "y"))
    kj = ("zh", "y")
    return jax.shard_map(
        local,
        mesh=fine,
        in_specs=(
            P("qi", None, kj, None),
            P(NOISE, "qi", None),
            P(NOISE, None, kj, None),
            P(NOISE, None, kj, None),
            P(NOISE, "qi", None),
            P(),
            P(),
            P(),
            P(),
            P(),
            P(),
        ),
        out_specs=(
            P(NOISE, ("qi", "zh", "y"), None),
            P(NOISE, ("qi", "zh", "y"), None),
            P(NOISE, ("qi", "zh", "y"), None),
            P("qi", NOISE, None, None, kj, None),
            P(),
            P(),
            P(),
            P(),
            P(),
            P(),
        ),
        check_vma=False,
    )
```
